32 devices in a mesh: grp: 2 (over y), blk: 4 (over z), ch: 2 (over x), sub: 2 (over core).
Axes of the slice: x: 2, y: 2, z: 4, core: 2. Of those that a mesh axis runs over, the one named last changes fastest.
Arguments:
- pair_act: bfloat16 [64, 32, 128], P(('grp', 'blk', 'ch', 'sub')), parts along dimension 0, may hold values from -6 to 6
- pair_grad: bfloat16 [64, 32, 128], P(('grp', 'blk', 'ch', 'sub')), parts along dimension 0, may hold values from -6 to 6
- pair_mask: int32 [64, 32], P(('grp', 'blk', 'ch', 'sub')), parts along dimension 0, may hold values from 0 to 1, as said below
- w_in: bfloat16 [128, 640], replicated, may hold values from -0.5 to 0.5
- w_out: bfloat16 [128, 128], replicated, may hold values from -0.5 to 0.5
- gain_in: float32 [128], replicated, may hold values from 0.5 to 1.5
- bias_in: float32 [128], replicated, may hold values from -2.5 to 2.5
- gain_mid: float32 [128], replicated, may hold values from 0.5 to 1.5
- bias_mid: float32 [128], replicated, may hold values from -2.5 to 2.5
Outputs:
- d_pair: bfloat16 [64, 32, 128], P(('grp', 'blk', 'ch', 'sub')), parts along dimension 0
- d_w_in: float32 [256, 640], P('grp'), parts along dimension 0
- d_w_out: float32 [256, 128], P('grp'), parts along dimension 0
- d_gain_in: float32 [256], P('grp'), parts along dimension 0
- d_bias_in: float32 [256], P('grp'), parts along dimension 0
- d_gain_mid: float32 [256], P('grp'), parts along dimension 0
- d_bias_mid: float32 [256], P('grp'), parts along dimension 0
The draws below stay inside these ranges and needn't reach their ends.
There are 2 independent parts, one for each index of `grp`. The reference program is written for one: setup_inputs(seed, part) draws one part's arguments, and reference() takes and returns one part's arrays. A program takes and returns all parts, laid end to end along the dimension named above; an argument that names none is the same for every part. Nothing has to cross between parts.
Inputs may be any that keep to these rules, and one draw needn't show every extreme that they name: pair_mask[i, j] = v[i] v[j] for one 0/1 vector v over the 32 tokens whose ones all come before its zeros, with at least 16 ones and at least one zero.
All inputs are finite; a program needn't handle non-finite values.
Results may differ from the reference program's by a relative error of at most 0.0089.
Values may be sent and summed in bfloat16 or wider, within the bound.
A program may use at most 64 MiB of HBM per device.

```python
import jax
import jax.numpy as jnp
from jax import lax

C = 128
H = 128
N = 32


def draw_pair_mask(key, part):
    key = jax.random.fold_in(key, 7)
    count = jax.random.randint(key, (), N // 2, N)
    valid = (jnp.arange(N) < count).astype(jnp.int32)
    return valid[:, None] * valid[None, :]


def level_of(stream_key, extent, pieces, smallest, largest):
    loudness, own = 1.0, jax.random.fold_in(stream_key, 6)
    for dim, shards_of in pieces:
        draws = jnp.exp(jax.random.uniform(jax.random.fold_in(own, dim), (shards_of,), jnp.float32, smallest / len(pieces), largest / len(pieces)))
        loudness = loudness * jnp.repeat(draws, extent[dim] // shards_of).reshape([-1 if axis == dim else 1 for axis in range(len(extent))])
    return loudness


def gaussian(stream_key, extent, deviation, reach, shards=(), dtype=jnp.bfloat16):
    drawn = deviation * jax.random.normal(stream_key, extent, jnp.float32)
    if shards:
        drawn = drawn * level_of(stream_key, extent, shards, -0.22, 0.18)
    return jnp.clip(drawn, -reach, reach).astype(dtype)


def setup_inputs(seed: int = 0, part: int = 0) -> dict:
    splits = jax.random.split(jax.random.key(seed), 10)
    part_splits = jax.random.split(jax.random.fold_in(splits[9], part), 10)
    pair_act = gaussian(part_splits[0], (N, N, C), 1.0, 6.0, ((0, 16),))
    pair_grad = gaussian(part_splits[1], (N, N, C), 1.0, 6.0, ((0, 16),))
    pair_mask = draw_pair_mask(jax.random.fold_in(jax.random.fold_in(splits[9], part), 71), part)
    w_in = gaussian(splits[3], (C, 4 * H + C), C ** -0.5, 0.5)
    w_out = gaussian(splits[4], (H, C), H ** -0.5, 0.5)
    gain_in = jnp.clip(1.0 + 0.1 * jax.random.normal(splits[5], (C,), jnp.float32), 0.5, 1.5)
    bias_in = gaussian(splits[6], (C,), 0.3, 2.5, (), jnp.float32)
    gain_mid = jnp.clip(1.0 + 0.1 * jax.random.normal(splits[7], (H,), jnp.float32), 0.5, 1.5)
    bias_mid = gaussian(splits[8], (H,), 0.3, 2.5, (), jnp.float32)
    return dict(pair_act=pair_act, pair_grad=pair_grad, pair_mask=pair_mask, w_in=w_in, w_out=w_out, gain_in=gain_in, bias_in=bias_in, gain_mid=gain_mid, bias_mid=bias_mid)


def norm_parts(values):
    center = values - lax.optimization_barrier(jnp.mean(values, axis=-1, keepdims=True))
    inverse = lax.rsqrt(lax.optimization_barrier(jnp.mean(center * center, axis=-1, keepdims=True)) + 1e-05)
    return (center * inverse, inverse)

def norm_back(upstream, normed, inverse):
    first = lax.optimization_barrier(jnp.mean(upstream, axis=-1, keepdims=True))
    second = lax.optimization_barrier(jnp.mean(upstream * normed, axis=-1, keepdims=True))
    return inverse * (upstream - first - normed * second)

def reference(pair_act, pair_grad, pair_mask, w_in, w_out, gain_in, bias_in, gain_mid, bias_mid):
    normed, inverse = norm_parts(pair_act.astype(jnp.float32))
    x_low = (normed * gain_in + bias_in).astype(jnp.bfloat16)
    flat_x = x_low.reshape(N * N, C)
    proj = jnp.dot(flat_x, w_in, preferred_element_type=jnp.float32).reshape(N, N, 4 * H + C)
    maskf = pair_mask.astype(jnp.float32)[:, :, None]
    sig_a = jax.nn.sigmoid(proj[..., :H])
    val_a = proj[..., H:2 * H]
    sig_b = jax.nn.sigmoid(proj[..., 2 * H:3 * H])
    val_b = proj[..., 3 * H:4 * H]
    sig_g = jax.nn.sigmoid(proj[..., 4 * H:])
    fac_a = lax.optimization_barrier((maskf * sig_a * val_a).astype(jnp.bfloat16))
    fac_b = lax.optimization_barrier((maskf * sig_b * val_b).astype(jnp.bfloat16))
    left = jnp.transpose(fac_a, (2, 0, 1)).astype(jnp.float32)
    right = jnp.transpose(fac_b, (2, 0, 1)).astype(jnp.float32)
    prod_t = jnp.einsum('hki,hkj->hij', left, right)
    prod = lax.optimization_barrier(jnp.transpose(prod_t, (1, 2, 0)).astype(jnp.bfloat16))
    mid, inverse_mid = norm_parts(prod.astype(jnp.float32))
    y_low = (mid * gain_mid + bias_mid).astype(jnp.bfloat16)
    flat_y = y_low.reshape(N * N, H)
    outp = jnp.dot(flat_y, w_out, preferred_element_type=jnp.float32).reshape(N, N, C)
    upstream = pair_grad.astype(jnp.float32)
    d_out = (upstream * sig_g).astype(jnp.bfloat16)
    d_sig = upstream * outp
    flat_d = d_out.reshape(N * N, C)
    d_w_out = jnp.dot(flat_y.T, flat_d, preferred_element_type=jnp.float32) / N
    d_mid = jnp.dot(flat_d, w_out.T, preferred_element_type=jnp.float32).reshape(N, N, H)
    d_gain_mid = lax.optimization_barrier(jnp.sum(d_mid * mid, axis=(0, 1))) / N
    d_bias_mid = lax.optimization_barrier(jnp.sum(d_mid, axis=(0, 1))) / N
    d_prod = lax.optimization_barrier(norm_back(d_mid * gain_mid, mid, inverse_mid).astype(jnp.bfloat16))
    d_prod_t = jnp.transpose(d_prod, (2, 0, 1)).astype(jnp.float32)
    grad_a_t = jnp.einsum('hkj,hij->hki', right, d_prod_t)
    grad_b_t = jnp.einsum('hki,hij->hkj', left, d_prod_t)
    grad_a = lax.optimization_barrier(jnp.transpose(grad_a_t, (1, 2, 0)).astype(jnp.bfloat16)).astype(jnp.float32)
    grad_b = lax.optimization_barrier(jnp.transpose(grad_b_t, (1, 2, 0)).astype(jnp.bfloat16)).astype(jnp.float32)
    d_gate_a = grad_a * maskf * val_a * sig_a * (1.0 - sig_a)
    d_val_a = grad_a * maskf * sig_a
    d_gate_b = grad_b * maskf * val_b * sig_b * (1.0 - sig_b)
    d_val_b = grad_b * maskf * sig_b
    d_gate_g = d_sig * sig_g * (1.0 - sig_g)
    d_proj = jnp.concatenate([d_gate_a, d_val_a, d_gate_b, d_val_b, d_gate_g], axis=-1).astype(jnp.bfloat16)
    flat_p = d_proj.reshape(N * N, 4 * H + C)
    d_w_in = jnp.dot(flat_x.T, flat_p, preferred_element_type=jnp.float32) / N
    d_x = jnp.dot(flat_p, w_in.T, preferred_element_type=jnp.float32).reshape(N, N, C)
    d_gain_in = lax.optimization_barrier(jnp.sum(d_x * normed, axis=(0, 1))) / N
    d_bias_in = lax.optimization_barrier(jnp.sum(d_x, axis=(0, 1))) / N
    d_pair = norm_back(d_x * gain_in, normed, inverse).astype(jnp.bfloat16)
    return (d_pair, d_w_in, d_w_out, d_gain_in, d_bias_in, d_gain_mid, d_bias_mid)
```

```python
import functools

import jax
import jax.numpy as jnp
from jax import lax
from jax.experimental import pallas as pl
from jax.experimental.pallas import tpu as pltpu
from jax.sharding import PartitionSpec as P


def norm_parts(values):
    center = values - jnp.mean(values, axis=-1, keepdims=True)
    inverse = lax.rsqrt(jnp.mean(center * center, axis=-1, keepdims=True) + 1e-05)
    return (center * inverse, inverse)


def norm_back(upstream, normed, inverse):
    first = jnp.mean(upstream, axis=-1, keepdims=True)
    second = jnp.mean(upstream * normed, axis=-1, keepdims=True)
    return inverse * (upstream - first - normed * second)


def shards(pair_act, pair_grad, pair_mask, w_in, w_out, gain_in, bias_in, gain_mid, bias_mid):
    rows, width, chan = pair_act.shape
    hidden = w_out.shape[0]
    normed, inverse = norm_parts(pair_act.astype(jnp.float32))
    x_low = (normed * gain_in + bias_in).astype(jnp.bfloat16)
    flat_x = x_low.reshape(rows * width, chan)
    proj = jnp.dot(flat_x, w_in, preferred_element_type=jnp.float32).reshape(rows, width, -1)
    maskf = pair_mask.astype(jnp.float32)[:, :, None]
    sig_a = jax.nn.sigmoid(proj[..., :hidden])
    val_a = proj[..., hidden : 2 * hidden]
    sig_b = jax.nn.sigmoid(proj[..., 2 * hidden : 3 * hidden])
    val_b = proj[..., 3 * hidden : 4 * hidden]
    sig_g = jax.nn.sigmoid(proj[..., 4 * hidden :])
    fac_a = (maskf * sig_a * val_a).astype(jnp.bfloat16)
    fac_b = (maskf * sig_b * val_b).astype(jnp.bfloat16)
    stacked = jnp.transpose(jnp.stack([fac_a, fac_b]), (0, 3, 1, 2))
    grouped = lax.all_to_all(stacked, ("ch", "sub"), split_axis=1, concat_axis=2, tiled=True)
    left_loc = grouped[0]
    right_loc = grouped[1]
    stripe = left_loc.shape[1]
    own_start = lax.axis_index("blk") * stripe
    columns = lax.dynamic_slice_in_dim(
        lax.all_gather(left_loc, "blk", axis=1, tiled=True), own_start, stripe, 2
    )
    total = jnp.einsum(
        "hki,hkj->hij",
        columns,
        lax.all_gather(right_loc, "blk", axis=1, tiled=True),
        preferred_element_type=jnp.float32,
    )
    returned_prod = lax.all_to_all(
        total.astype(jnp.bfloat16), ("ch", "sub"), split_axis=1, concat_axis=0, tiled=True
    )
    prod = jnp.transpose(returned_prod, (1, 2, 0)).astype(jnp.float32)
    mid, inverse_mid = norm_parts(prod)
    y_low = (mid * gain_mid + bias_mid).astype(jnp.bfloat16)
    flat_y = y_low.reshape(rows * width, hidden)
    outp = jnp.dot(flat_y, w_out, preferred_element_type=jnp.float32).reshape(rows, width, chan)
    upstream = pair_grad.astype(jnp.float32)
    d_out = (upstream * sig_g).astype(jnp.bfloat16)
    d_sig = upstream * outp
    flat_d = d_out.reshape(rows * width, chan)
    dw_out_part = jnp.dot(flat_y.T, flat_d, preferred_element_type=jnp.float32)
    d_mid = jnp.dot(flat_d, w_out.T, preferred_element_type=jnp.float32).reshape(
        rows, width, hidden
    )
    dgain_mid_part = jnp.sum(d_mid * mid, axis=(0, 1))
    dbias_mid_part = jnp.sum(d_mid, axis=(0, 1))
    mid_totals = lax.psum((dw_out_part, dgain_mid_part, dbias_mid_part), ("blk", "ch", "sub"))
    d_prod = norm_back(d_mid * gain_mid, mid, inverse_mid).astype(jnp.bfloat16)
    d_groups = lax.all_to_all(
        jnp.transpose(d_prod, (2, 0, 1)), ("ch", "sub"), split_axis=0, concat_axis=1, tiled=True
    )
    piece = lax.all_gather(d_groups, "blk", axis=1, tiled=True)
    part_left = jnp.einsum("hkj,hij->hki", right_loc, piece, preferred_element_type=jnp.float32)
    grad_left = part_left
    grad_right = jnp.einsum("hki,hij->hkj", left_loc, piece, preferred_element_type=jnp.float32)
    grad_left, grad_right = (grad_left, grad_right)
    both_grads = jnp.stack([grad_left, grad_right]).astype(jnp.bfloat16)
    returned_grads = lax.all_to_all(
        both_grads, ("ch", "sub"), split_axis=2, concat_axis=1, tiled=True
    )
    pair_grads = jnp.transpose(returned_grads, (0, 2, 3, 1)).astype(jnp.float32)
    grad_a = pair_grads[0]
    grad_b = pair_grads[1]
    d_gate_a = grad_a * maskf * val_a * sig_a * (1.0 - sig_a)
    d_val_a = grad_a * maskf * sig_a
    d_gate_b = grad_b * maskf * val_b * sig_b * (1.0 - sig_b)
    d_val_b = grad_b * maskf * sig_b
    d_gate_g = d_sig * sig_g * (1.0 - sig_g)
    d_proj = jnp.concatenate([d_gate_a, d_val_a, d_gate_b, d_val_b, d_gate_g], axis=-1).astype(
        jnp.bfloat16
    )
    flat_p = d_proj.reshape(rows * width, -1)
    dw_in_part = jnp.dot(flat_x.T, flat_p, preferred_element_type=jnp.float32)
    d_x = jnp.dot(flat_p, w_in.T, preferred_element_type=jnp.float32).reshape(rows, width, chan)
    dgain_in_part = jnp.sum(d_x * normed, axis=(0, 1))
    dbias_in_part = jnp.sum(d_x, axis=(0, 1))
    d_pair = norm_back(d_x * gain_in, normed, inverse).astype(jnp.bfloat16)
    scale = 1.0 / width
    in_totals = lax.psum((dw_in_part, dgain_in_part, dbias_in_part), ("blk", "ch", "sub"))
    sums = (in_totals[0], in_totals[1], in_totals[2], mid_totals[0], mid_totals[1], mid_totals[2])
    return (
        d_pair,
        sums[0] * scale,
        sums[3] * scale,
        sums[1] * scale,
        sums[2] * scale,
        sums[4] * scale,
        sums[5] * scale,
    )


MESH = pl.DeviceIdType.MESH
PAD = 16
VMEM_BYTES = 48 * 1024 * 1024


def flat_slot(sizes, blk, ch, sub):
    return (blk * sizes[1] + ch) * sizes[2] + sub


def gather_kernel(sizes, act_ref, grad_ref, mask_ref, ga_ref, gg_ref, send_sem, recv_sem):
    nz, nx, nc = sizes
    z, x, c = lax.axis_index("blk"), lax.axis_index("ch"), lax.axis_index("sub")
    y = lax.axis_index("grp")
    pairs = act_ref.shape[0]
    width = mask_ref.shape[1]
    me = flat_slot(sizes, z, x, c)
    barrier = pltpu.get_barrier_semaphore()
    peers_z = [(y, lax.rem(z + s, nz), x, c) for s in range(1, nz)]
    peers_x = [(y, z, lax.rem(x + s, nx), c) for s in range(1, nx)]
    peers_c = [(y, z, x, lax.rem(c + s, nc)) for s in range(1, nc)]
    peers = peers_z + peers_x + peers_c
    for peer in peers:
        pl.semaphore_signal(barrier, inc=1, device_id=peer, device_id_type=MESH)
    ga_ref[me, :pairs, :] = act_ref[...]
    ga_ref[me, pairs:, :] = jnp.zeros((PAD, act_ref.shape[1]), jnp.bfloat16)
    ga_ref[me, pairs:, :width] = jnp.broadcast_to(
        mask_ref[0:1, :].astype(jnp.float32), (PAD, width)
    ).astype(jnp.bfloat16)
    gg_ref[me] = grad_ref[...]
    pl.semaphore_wait(barrier, len(peers))

    bufs = (ga_ref, gg_ref)
    copies = []
    counts = [0, 0]

    def push(which, slot, peer):
        buf = bufs[which]
        copy = pltpu.make_async_remote_copy(
            src_ref=buf.at[slot],
            dst_ref=buf.at[slot],
            send_sem=send_sem.at[which, counts[which]],
            recv_sem=recv_sem.at[which, slot],
            device_id=peer,
            device_id_type=MESH,
        )
        counts[which] += 1
        copy.start()
        copies.append(copy)

    def arrived(which, slot):
        buf = bufs[which]
        pltpu.make_async_remote_copy(
            src_ref=buf.at[slot],
            dst_ref=buf.at[slot],
            send_sem=send_sem.at[which, 0],
            recv_sem=recv_sem.at[which, slot],
            device_id=peers[0],
            device_id_type=MESH,
        ).wait_recv()

    for which in (0, 1):
        for peer in peers_z:
            push(which, me, peer)
        for peer in peers_x + peers_c:
            push(which, me, peer)
    order_z = [lax.rem(z + s, nz) for s in range(1, nz)]
    for which in (0, 1):
        for zz in order_z:
            slot = flat_slot(sizes, zz, x, c)
            arrived(which, slot)
            for peer in peers_x + peers_c:
                push(which, slot, peer)
        for s in range(1, nx):
            xx = lax.rem(x + s, nx)
            for zz in [z] + order_z:
                slot = flat_slot(sizes, zz, xx, c)
                arrived(which, slot)
                for peer in peers_c:
                    push(which, slot, peer)
    for which in (0, 1):
        for s in range(1, nc):
            cc = lax.rem(c + s, nc)
            for xx in [x] + [lax.rem(x + q, nx) for q in range(1, nx)]:
                for zz in [z] + order_z:
                    arrived(which, flat_slot(sizes, zz, xx, cc))
    for copy in copies:
        copy.wait_send()


def lane_mean(values):
    return jnp.mean(values, axis=-1, keepdims=True)


def norm_rows(values):
    center = values - lane_mean(values)
    inverse = lax.rsqrt(lane_mean(center * center) + 1e-05)
    return center * inverse, inverse


def sigm(values):
    return 0.5 * jnp.tanh(0.5 * values) + 0.5


def dot_t(left, right):
    return lax.dot_general(left, right, (((1,), (1,)), ((), ())), preferred_element_type=jnp.float32)


def t_dot(left, right):
    return lax.dot_general(left, right, (((0,), (0,)), ((), ())), preferred_element_type=jnp.float32)


def outer_sum(length, row_of, vec_of, width, chan, block):
    step = 4

    def body(t, acc):
        acc = list(acc)
        for s in range(step):
            q = t * step + s
            vec = vec_of(q)
            for p in range(block):
                acc[p] = acc[p] + row_of(p, q) * vec
        return tuple(acc)

    zero = jnp.zeros((width, chan), jnp.float32)
    return lax.fori_loop(0, length // step, body, (zero,) * block)


def compute_kernel(
    sizes, rows, width,
    ga_ref, gg_ref, w_in_ref, w_out_ref, gain_in_ref, bias_in_ref, gain_mid_ref, bias_mid_ref,
    d_pair_ref, dw_in_ref, dw_out_ref, dgain_in_ref, dbias_in_ref, dgain_mid_ref, dbias_mid_ref,
    xs, nrm, fa, fb, ca, cb, qa, qb, sg, ys, dos, dp, dpr, dxs, vc,
):
    nz, nx, nc = sizes
    slots = nz * nx * nc
    pairs = rows * width
    chan = w_out_ref.shape[1]
    hid = w_out_ref.shape[0]
    scale = 1.0 / width
    me = flat_slot(sizes, lax.axis_index("blk"), lax.axis_index("ch"), lax.axis_index("sub"))

    lane_v = ga_ref[0, pairs:, :].astype(jnp.float32)[0:1, :]
    at_row = lax.broadcasted_iota(jnp.int32, (width, chan), 0)
    at_lane = lax.broadcasted_iota(jnp.int32, (width, chan), 1)
    diag = jnp.where(at_row == at_lane, jnp.broadcast_to(lane_v, (width, chan)), 0.0)
    vc[...] = jnp.dot(
        diag.astype(jnp.bfloat16), jnp.ones((chan, chan), jnp.bfloat16),
        preferred_element_type=jnp.float32,
    )
    gain_in, bias_in = gain_in_ref[...], bias_in_ref[...]
    gain_mid, bias_mid = gain_mid_ref[...], bias_mid_ref[...]

    per = 2

    def project(t, carry):
        act = jnp.concatenate([ga_ref[t * per + s, :pairs, :] for s in range(per)], axis=0)
        size = per * pairs
        here = pl.ds(pl.multiple_of(t * size, size), size)
        normed, _ = norm_rows(act.astype(jnp.float32))
        x_low = (normed * gain_in + bias_in).astype(jnp.bfloat16)
        nrm[here, :] = normed
        xs[here, :] = x_low
        cols = vc[...]
        mask = jnp.concatenate(
            [cols * vc[pl.ds(t * per * rows + r, 1), :] for r in range(per * rows)], axis=0
        )
        proj = jnp.dot(x_low, w_in_ref[...], preferred_element_type=jnp.float32)
        for at, fac, coef, gate in ((0, fa, ca, qa), (2, fb, cb, qb)):
            sig = sigm(proj[:, at * hid : (at + 1) * hid])
            val = proj[:, (at + 1) * hid : (at + 2) * hid]
            masked = mask * sig
            full = masked * val
            fac[here, :] = full.astype(jnp.bfloat16).astype(jnp.float32)
            coef[here, :] = masked
            gate[here, :] = full * (1.0 - sig)
        sg[here, :] = sigm(proj[:, 4 * hid :])
        return carry

    lax.fori_loop(0, slots // per, project, 0)

    block = 8
    big = block * width

    def middle(ib, sums):
        dgain, dbias = sums
        base = ib * block
        total = outer_sum(
            width,
            lambda p, k: fa[pl.ds(k * width + base + p, 1), :],
            lambda k: fb[pl.ds(pl.multiple_of(k * width, width), width), :],
            width, hid, block,
        )
        here = pl.ds(pl.multiple_of(base * width, big), big)
        prod = jnp.concatenate(total, axis=0).astype(jnp.bfloat16).astype(jnp.float32)
        mid, inverse = norm_rows(prod)
        y_low = (mid * gain_mid + bias_mid).astype(jnp.bfloat16)
        ys[here, :] = y_low
        per_block = block // rows
        upstream = jnp.concatenate(
            [gg_ref[ib * per_block + s] for s in range(per_block)], axis=0
        ).astype(jnp.float32)
        sig = sg[here, :]
        outp = jnp.dot(y_low, w_out_ref[...], preferred_element_type=jnp.float32)
        d_out = (upstream * sig).astype(jnp.bfloat16)
        dos[here, :] = d_out
        dpr[here, 4 * hid :] = (upstream * outp * sig * (1.0 - sig)).astype(jnp.bfloat16)
        d_mid = dot_t(d_out, w_out_ref[...])
        dgain = dgain + jnp.sum(d_mid * mid, axis=0, keepdims=True)
        dbias = dbias + jnp.sum(d_mid, axis=0, keepdims=True)
        u = d_mid * gain_mid
        d_prod = inverse * (u - lane_mean(u) - mid * lane_mean(u * mid))
        dp[here, :] = d_prod.astype(jnp.bfloat16).astype(jnp.float32)
        return dgain, dbias

    none = jnp.zeros((1, hid), jnp.float32)
    dgain, dbias = lax.fori_loop(0, width // block, middle, (none, none))
    dgain_mid_ref[...] = dgain * scale
    dbias_mid_ref[...] = dbias * scale
    dw_out_ref[...] = t_dot(ys[...], dos[...]) * scale

    def back(kb, sums):
        dgain, dbias = sums
        base = kb * block
        here = pl.ds(pl.multiple_of(base * width, big), big)
        left = outer_sum(
            width,
            lambda p, j: fb[pl.ds((base + p) * width + j, 1), :],
            lambda j: dp[pl.ds(j, width, stride=width), :],
            width, hid, block,
        )
        grad = jnp.concatenate(left, axis=0).astype(jnp.bfloat16).astype(jnp.float32)
        dpr[here, :hid] = (grad * qa[here, :]).astype(jnp.bfloat16)
        dpr[here, hid : 2 * hid] = (grad * ca[here, :]).astype(jnp.bfloat16)
        right = outer_sum(
            width,
            lambda p, i: fa[pl.ds((base + p) * width + i, 1), :],
            lambda i: dp[pl.ds(pl.multiple_of(i * width, width), width), :],
            width, hid, block,
        )
        grad = jnp.concatenate(right, axis=0).astype(jnp.bfloat16).astype(jnp.float32)
        dpr[here, 2 * hid : 3 * hid] = (grad * qb[here, :]).astype(jnp.bfloat16)
        dpr[here, 3 * hid : 4 * hid] = (grad * cb[here, :]).astype(jnp.bfloat16)
        d_x = dot_t(dpr[here, :], w_in_ref[...])
        dxs[here, :] = d_x
        dgain = dgain + jnp.sum(d_x * nrm[here, :], axis=0, keepdims=True)
        dbias = dbias + jnp.sum(d_x, axis=0, keepdims=True)
        return dgain, dbias

    none = jnp.zeros((1, chan), jnp.float32)
    dgain, dbias = lax.fori_loop(0, width // block, back, (none, none))
    dgain_in_ref[...] = dgain * scale
    dbias_in_ref[...] = dbias * scale
    dw_in_ref[...] = t_dot(xs[...], dpr[...]) * scale
    _, inverse = norm_rows(ga_ref[me, :pairs, :].astype(jnp.float32))
    own = pl.ds(pl.multiple_of(me * pairs, pairs), pairs)
    normed = nrm[own, :]
    v = dxs[own, :] * gain_in
    d_pair_ref[...] = (inverse * (v - lane_mean(v) - normed * lane_mean(v * normed))).astype(
        jnp.bfloat16
    )


def fused(sizes, pair_act, pair_grad, pair_mask, w_in, w_out, gain_in, bias_in, gain_mid, bias_mid):
    rows, width, chan = pair_act.shape
    hid = w_out.shape[0]
    pairs = rows * width
    slots = sizes[0] * sizes[1] * sizes[2]
    sends = sizes[0] - 1 + sizes[0] * (sizes[1] - 1) + sizes[0] * sizes[1] * (sizes[2] - 1)
    vmem = pl.BlockSpec(memory_space=pltpu.VMEM)
    ga, gg = pl.pallas_call(
        functools.partial(gather_kernel, sizes),
        out_shape=(
            jax.ShapeDtypeStruct((slots, pairs + PAD, chan), jnp.bfloat16),
            jax.ShapeDtypeStruct((slots, pairs, chan), jnp.bfloat16),
        ),
        in_specs=[vmem] * 3,
        out_specs=(vmem, vmem),
        scratch_shapes=[
            pltpu.SemaphoreType.DMA((2, sends)),
            pltpu.SemaphoreType.DMA((2, slots)),
        ],
        compiler_params=pltpu.CompilerParams(
            collective_id=0, has_side_effects=True, vmem_limit_bytes=VMEM_BYTES
        ),
    )(pair_act.reshape(pairs, chan), pair_grad.reshape(pairs, chan), pair_mask)
    full = slots * pairs
    f32, low = jnp.float32, jnp.bfloat16
    out = pl.pallas_call(
        functools.partial(compute_kernel, sizes, rows, width),
        out_shape=(
            jax.ShapeDtypeStruct((pairs, chan), low),
            jax.ShapeDtypeStruct(w_in.shape, f32),
            jax.ShapeDtypeStruct(w_out.shape, f32),
            jax.ShapeDtypeStruct((1, chan), f32),
            jax.ShapeDtypeStruct((1, chan), f32),
            jax.ShapeDtypeStruct((1, hid), f32),
            jax.ShapeDtypeStruct((1, hid), f32),
        ),
        in_specs=[vmem] * 8,
        out_specs=(vmem,) * 7,
        scratch_shapes=[
            pltpu.VMEM((full, chan), low),
            pltpu.VMEM((full, chan), f32),
        ]
        + [pltpu.VMEM((full, hid), f32)] * 6
        + [
            pltpu.VMEM((full, chan), f32),
            pltpu.VMEM((full, hid), low),
            pltpu.VMEM((full, chan), low),
            pltpu.VMEM((full, hid), f32),
            pltpu.VMEM((full, w_in.shape[1]), low),
            pltpu.VMEM((full, chan), f32),
            pltpu.VMEM((width, hid), f32),
        ],
        compiler_params=pltpu.CompilerParams(vmem_limit_bytes=VMEM_BYTES),
    )(
        ga, gg, w_in, w_out, gain_in.reshape(1, chan), bias_in.reshape(1, chan),
        gain_mid.reshape(1, hid), bias_mid.reshape(1, hid),
    )
    return (out[0].reshape(rows, width, chan), out[1], out[2]) + tuple(
        piece.reshape(-1) for piece in out[3:]
    )


def choose(mesh, *args):
    rows, width, chan = args[0].shape
    sizes = (mesh.shape["blk"], mesh.shape["ch"], mesh.shape["sub"])
    fits = width * width * chan * 64 <= VMEM_BYTES // 2
    whole = width % 32 == 0 and 8 % rows == 0 and chan == 128 and args[4].shape[0] == 128
    if fits and whole and rows * sizes[0] * sizes[1] * sizes[2] == width:
        return fused(sizes, *args)
    return shards(*args)


def solution(mesh):
    in_specs = (
        P(("grp", "blk", "ch", "sub"), None, None),
        P(("grp", "blk", "ch", "sub"), None, None),
        P(("grp", "blk", "ch", "sub"), None),
        P(),
        P(),
        P(),
        P(),
        P(),
        P(),
    )
    out_specs = (
        P(("grp", "blk", "ch", "sub"), None, None),
        P("grp", None),
        P("grp", None),
        P("grp"),
        P("grp"),
        P("grp"),
        P("grp"),
    )
    body = functools.partial(choose, mesh)
    return jax.shard_map(body, mesh=mesh, in_specs=in_specs, out_specs=out_specs, check_vma=False)
```

```python
import functools

import jax
import jax.numpy as jnp
from jax import lax
from jax.experimental import pallas as pl
from jax.experimental.pallas import tpu as pltpu
from jax.sharding import PartitionSpec as P


def norm_parts(values):
    center = values - jnp.mean(values, axis=-1, keepdims=True)
    inverse = lax.rsqrt(jnp.mean(center * center, axis=-1, keepdims=True) + 1e-05)
    return (center * inverse, inverse)


def norm_back(upstream, normed, inverse):
    first = jnp.mean(upstream, axis=-1, keepdims=True)
    second = jnp.mean(upstream * normed, axis=-1, keepdims=True)
    return inverse * (upstream - first - normed * second)


def shards(pair_act, pair_grad, pair_mask, w_in, w_out, gain_in, bias_in, gain_mid, bias_mid):
    rows, width, chan = pair_act.shape
    hidden = w_out.shape[0]
    normed, inverse = norm_parts(pair_act.astype(jnp.float32))
    x_low = (normed * gain_in + bias_in).astype(jnp.bfloat16)
    flat_x = x_low.reshape(rows * width, chan)
    proj = jnp.dot(flat_x, w_in, preferred_element_type=jnp.float32).reshape(rows, width, -1)
    maskf = pair_mask.astype(jnp.float32)[:, :, None]
    sig_a = jax.nn.sigmoid(proj[..., :hidden])
    val_a = proj[..., hidden : 2 * hidden]
    sig_b = jax.nn.sigmoid(proj[..., 2 * hidden : 3 * hidden])
    val_b = proj[..., 3 * hidden : 4 * hidden]
    sig_g = jax.nn.sigmoid(proj[..., 4 * hidden :])
    fac_a = (maskf * sig_a * val_a).astype(jnp.bfloat16)
    fac_b = (maskf * sig_b * val_b).astype(jnp.bfloat16)
    stacked = jnp.transpose(jnp.stack([fac_a, fac_b]), (0, 3, 1, 2))
    grouped = lax.all_to_all(stacked, ("ch", "sub"), split_axis=1, concat_axis=2, tiled=True)
    left_loc = grouped[0]
    right_loc = grouped[1]
    stripe = left_loc.shape[1]
    own_start = lax.axis_index("blk") * stripe
    columns = lax.dynamic_slice_in_dim(
        lax.all_gather(left_loc, "blk", axis=1, tiled=True), own_start, stripe, 2
    )
    total = jnp.einsum(
        "hki,hkj->hij",
        columns,
        lax.all_gather(right_loc, "blk", axis=1, tiled=True),
        preferred_element_type=jnp.float32,
    )
    returned_prod = lax.all_to_all(
        total.astype(jnp.bfloat16), ("ch", "sub"), split_axis=1, concat_axis=0, tiled=True
    )
    prod = jnp.transpose(returned_prod, (1, 2, 0)).astype(jnp.float32)
    mid, inverse_mid = norm_parts(prod)
    y_low = (mid * gain_mid + bias_mid).astype(jnp.bfloat16)
    flat_y = y_low.reshape(rows * width, hidden)
    outp = jnp.dot(flat_y, w_out, preferred_element_type=jnp.float32).reshape(rows, width, chan)
    upstream = pair_grad.astype(jnp.float32)
    d_out = (upstream * sig_g).astype(jnp.bfloat16)
    d_sig = upstream * outp
    flat_d = d_out.reshape(rows * width, chan)
    dw_out_part = jnp.dot(flat_y.T, flat_d, preferred_element_type=jnp.float32)
    d_mid = jnp.dot(flat_d, w_out.T, preferred_element_type=jnp.float32).reshape(
        rows, width, hidden
    )
    dgain_mid_part = jnp.sum(d_mid * mid, axis=(0, 1))
    dbias_mid_part = jnp.sum(d_mid, axis=(0, 1))
    mid_totals = lax.psum((dw_out_part, dgain_mid_part, dbias_mid_part), ("blk", "ch", "sub"))
    d_prod = norm_back(d_mid * gain_mid, mid, inverse_mid).astype(jnp.bfloat16)
    d_groups = lax.all_to_all(
        jnp.transpose(d_prod, (2, 0, 1)), ("ch", "sub"), split_axis=0, concat_axis=1, tiled=True
    )
    piece = lax.all_gather(d_groups, "blk", axis=1, tiled=True)
    part_left = jnp.einsum("hkj,hij->hki", right_loc, piece, preferred_element_type=jnp.float32)
    grad_left = part_left
    grad_right = jnp.einsum("hki,hij->hkj", left_loc, piece, preferred_element_type=jnp.float32)
    grad_left, grad_right = (grad_left, grad_right)
    both_grads = jnp.stack([grad_left, grad_right]).astype(jnp.bfloat16)
    returned_grads = lax.all_to_all(
        both_grads, ("ch", "sub"), split_axis=2, concat_axis=1, tiled=True
    )
    pair_grads = jnp.transpose(returned_grads, (0, 2, 3, 1)).astype(jnp.float32)
    grad_a = pair_grads[0]
    grad_b = pair_grads[1]
    d_gate_a = grad_a * maskf * val_a * sig_a * (1.0 - sig_a)
    d_val_a = grad_a * maskf * sig_a
    d_gate_b = grad_b * maskf * val_b * sig_b * (1.0 - sig_b)
    d_val_b = grad_b * maskf * sig_b
    d_gate_g = d_sig * sig_g * (1.0 - sig_g)
    d_proj = jnp.concatenate([d_gate_a, d_val_a, d_gate_b, d_val_b, d_gate_g], axis=-1).astype(
        jnp.bfloat16
    )
    flat_p = d_proj.reshape(rows * width, -1)
    dw_in_part = jnp.dot(flat_x.T, flat_p, preferred_element_type=jnp.float32)
    d_x = jnp.dot(flat_p, w_in.T, preferred_element_type=jnp.float32).reshape(rows, width, chan)
    dgain_in_part = jnp.sum(d_x * normed, axis=(0, 1))
    dbias_in_part = jnp.sum(d_x, axis=(0, 1))
    d_pair = norm_back(d_x * gain_in, normed, inverse).astype(jnp.bfloat16)
    scale = 1.0 / width
    in_totals = lax.psum((dw_in_part, dgain_in_part, dbias_in_part), ("blk", "ch", "sub"))
    sums = (in_totals[0], in_totals[1], in_totals[2], mid_totals[0], mid_totals[1], mid_totals[2])
    return (
        d_pair,
        sums[0] * scale,
        sums[3] * scale,
        sums[1] * scale,
        sums[2] * scale,
        sums[4] * scale,
        sums[5] * scale,
    )


MESH = pl.DeviceIdType.MESH
PAD = 16
VMEM_BYTES = 32 * 1024 * 1024


def flat_slot(sizes, blk, ch, sub):
    return (blk * sizes[1] + ch) * sizes[2] + sub


def lane_mean(values):
    return jnp.mean(values, axis=-1, keepdims=True)


def norm_rows(values):
    center = values - lane_mean(values)
    inverse = lax.rsqrt(lane_mean(center * center) + 1e-05)
    return center * inverse, inverse


def sigm(values):
    return 0.5 * jnp.tanh(0.5 * values) + 0.5


def dot_t(left, right):
    return lax.dot_general(left, right, (((1,), (1,)), ((), ())), preferred_element_type=jnp.float32)


def t_dot(left, right):
    return lax.dot_general(left, right, (((0,), (0,)), ((), ())), preferred_element_type=jnp.float32)


def outer_sum(length, row_of, vec_of, width, chan, block):
    step = 4

    def body(t, acc):
        acc = list(acc)
        for s in range(step):
            q = t * step + s
            vec = vec_of(q)
            for p in range(block):
                acc[p] = acc[p] + row_of(p, q) * vec
        return tuple(acc)

    zero = jnp.zeros((width, chan), jnp.float32)
    return lax.fori_loop(0, length // step, body, (zero,) * block)


def front_kernel(
    sizes, rows, width,
    act_hbm, grad_hbm, mask_hbm, w_in_hbm, w_out_hbm, gain_in_ref, bias_in_ref, gain_mid_ref, bias_mid_ref,
    xs, nrm, fa, fb, ca, cb, qa, qb, dp, dpg, dw_out_ref, dgain_mid_ref, dbias_mid_ref,
    ga, gg, mask_ref, w_in_ref, w_out_ref, sg, ys, dos, in_sem, send_sem, recv_sem, core_send,
):
    nz, nx, nc = sizes
    chips = nz * nx
    pairs = rows * width
    chan = w_out_ref.shape[1]
    hid = w_out_ref.shape[0]
    scale = 1.0 / width
    z, x, c = lax.axis_index("blk"), lax.axis_index("ch"), lax.axis_index("sub")
    y = lax.axis_index("grp")
    me = flat_slot(sizes, z, x, c)
    barrier = pltpu.get_barrier_semaphore()
    others = [
        (lax.rem(z + s, nz), lax.rem(x + r, nx))
        for r in range(nx) for s in range(nz) if s or r
    ]
    peers = [(y, zz, xx, c) for zz, xx in others]
    cores = [(y, z, x, lax.rem(c + s, nc)) for s in range(1, nc)]
    for peer in peers + cores:
        pl.semaphore_signal(barrier, inc=1, device_id=peer, device_id_type=MESH)
    loads = [
        pltpu.make_async_copy(act_hbm, ga.at[me, pl.ds(0, pairs)], in_sem.at[0]),
        pltpu.make_async_copy(mask_hbm, mask_ref, in_sem.at[1]),
        pltpu.make_async_copy(grad_hbm, gg.at[me], in_sem.at[2]),
        pltpu.make_async_copy(w_in_hbm, w_in_ref, in_sem.at[3]),
        pltpu.make_async_copy(w_out_hbm, w_out_ref, in_sem.at[4]),
    ]
    for load in loads:
        load.start()
    loads[1].wait()
    ga[me, pairs:, :] = jnp.zeros((PAD, chan), jnp.bfloat16)
    mine = mask_ref[...].astype(jnp.float32)
    ga[me, pairs:, :width] = jnp.concatenate(
        [jnp.broadcast_to(mine[r : r + 1, :], (PAD // rows, width)) for r in range(rows)], axis=0
    ).astype(jnp.bfloat16)
    loads[0].wait()
    pl.semaphore_wait(barrier, len(peers) + len(cores))

    bufs = (ga, gg)

    def chip_copy(which, slot, n, peer):
        return pltpu.make_async_remote_copy(
            src_ref=bufs[which].at[slot], dst_ref=bufs[which].at[slot],
            send_sem=send_sem.at[which, n], recv_sem=recv_sem.at[which, slot],
            device_id=peer, device_id_type=MESH,
        )

    def core_copy(which, slot, n):
        return pltpu.make_async_remote_copy(
            src_ref=bufs[which].at[slot], dst_ref=bufs[which].at[slot],
            send_sem=core_send.at[which, n], recv_sem=recv_sem.at[which, slot],
            device_id=cores[n // chips], device_id_type=MESH,
        )

    def send_own(which):
        for n, peer in enumerate(peers):
            chip_copy(which, me, n, peer).start()
        for k in range(nc - 1):
            core_copy(which, me, k * chips).start()

    def take(which, n):
        zz, xx = others[n - 1]
        slot = flat_slot(sizes, zz, xx, c)
        chip_copy(which, slot, 0, peers[0]).wait_recv()
        for k in range(nc - 1):
            core_copy(which, slot, k * chips + n).start()

    def take_core(which, slot):
        chip_copy(which, slot, 0, peers[0]).wait_recv()

    send_own(0)
    gain_in, bias_in = gain_in_ref[...], bias_in_ref[...]
    gain_mid, bias_mid = gain_mid_ref[...], bias_mid_ref[...]
    at_row = lax.broadcasted_iota(jnp.int32, (width, chan), 0)
    at_lane = lax.broadcasted_iota(jnp.int32, (width, chan), 1)
    on_diag = at_row == at_lane
    ones = jnp.ones((chan, chan), jnp.bfloat16)

    def project(slots):
        act = jnp.concatenate([ga[s, :pairs, :] for s in slots], axis=0)
        lines = [ga[s, pairs:, :].astype(jnp.float32) for s in slots]
        diag = [
            jnp.where(on_diag, jnp.broadcast_to(line[r * (PAD // rows)][None, :], (width, chan)), 0.0)
            for line in lines for r in range(rows)
        ]
        mask = jnp.dot(
            jnp.concatenate(diag, axis=0).astype(jnp.bfloat16), ones,
            preferred_element_type=jnp.float32,
        )
        normed, _ = norm_rows(act.astype(jnp.float32))
        x_low = (normed * gain_in + bias_in).astype(jnp.bfloat16)

        def put(ref, value):
            for p, s in enumerate(slots):
                ref[pl.ds(pl.multiple_of(s * pairs, pairs), pairs), :] = value[
                    p * pairs : (p + 1) * pairs
                ]

        put(nrm, normed)
        put(xs, x_low)
        proj = jnp.dot(x_low, w_in_ref[...], preferred_element_type=jnp.float32)
        for at, fac, coef, gate in ((0, fa, ca, qa), (2, fb, cb, qb)):
            sig = sigm(proj[:, at * hid : (at + 1) * hid])
            val = proj[:, (at + 1) * hid : (at + 2) * hid]
            masked = mask * sig
            full = masked * val
            put(fac, full.astype(jnp.bfloat16).astype(jnp.float32))
            put(coef, masked)
            put(gate, full * (1.0 - sig))
        put(sg, sigm(proj[:, 4 * hid :]))

    loads[3].wait()
    loads[2].wait()
    for n in range(1, nz):
        take(0, n)
    send_own(1)
    for r in range(nx):
        if r:
            for n in range(r * nz, (r + 1) * nz):
                take(0, n)
        xx = lax.rem(x + r, nx)
        project([flat_slot(sizes, lax.rem(z + s, nz), xx, c) for s in range(nz)])
    for k in range(1, nc):
        cc = lax.rem(c + k, nc)
        for r in range(nx):
            xx = lax.rem(x + r, nx)
            slots = [flat_slot(sizes, lax.rem(z + s, nz), xx, cc) for s in range(nz)]
            for slot in slots:
                take_core(0, slot)
            project(slots)
    for n in range(1, chips):
        take(1, n)
    loads[4].wait()

    block = 8
    big = block * width

    def product(ib, carry):
        base = ib * block
        total = outer_sum(
            width,
            lambda p, k: fa[pl.ds(k * width + base + p, 1), :],
            lambda k: fb[pl.ds(pl.multiple_of(k * width, width), width), :],
            width, hid, block,
        )
        dp[pl.ds(pl.multiple_of(base * width, big), big), :] = jnp.concatenate(total, axis=0)
        return carry

    lax.fori_loop(0, width // block, product, 0)
    for k in range(1, nc):
        cc = lax.rem(c + k, nc)
        for zz, xx in [(z, x)] + others:
            take_core(1, flat_slot(sizes, zz, xx, cc))

    def middle(ib, sums):
        dgain, dbias = sums
        here = pl.ds(pl.multiple_of(ib * big, big), big)
        prod = dp[here, :].astype(jnp.bfloat16).astype(jnp.float32)
        mid, inverse = norm_rows(prod)
        y_low = (mid * gain_mid + bias_mid).astype(jnp.bfloat16)
        ys[here, :] = y_low
        per_block = block // rows
        upstream = jnp.concatenate(
            [gg[ib * per_block + s] for s in range(per_block)], axis=0
        ).astype(jnp.float32)
        sig = sg[here, :]
        outp = jnp.dot(y_low, w_out_ref[...], preferred_element_type=jnp.float32)
        d_out = (upstream * sig).astype(jnp.bfloat16)
        dos[here, :] = d_out
        dpg[here, :] = (upstream * outp * sig * (1.0 - sig)).astype(jnp.bfloat16)
        d_mid = dot_t(d_out, w_out_ref[...])
        dgain = dgain + jnp.sum(d_mid * mid, axis=0, keepdims=True)
        dbias = dbias + jnp.sum(d_mid, axis=0, keepdims=True)
        u = d_mid * gain_mid
        d_prod = inverse * (u - lane_mean(u) - mid * lane_mean(u * mid))
        dp[here, :] = d_prod.astype(jnp.bfloat16).astype(jnp.float32)
        return dgain, dbias

    none = jnp.zeros((1, hid), jnp.float32)
    dgain, dbias = lax.fori_loop(0, width // block, middle, (none, none))
    dgain_mid_ref[...] = dgain * scale
    dbias_mid_ref[...] = dbias * scale
    dw_out_ref[...] = t_dot(ys[...], dos[...]) * scale
    for which in (0, 1):
        for n, peer in enumerate(peers):
            chip_copy(which, me, n, peer).wait_send()
        for n in range((nc - 1) * chips):
            core_copy(which, me, n).wait_send()


def back_kernel(
    sizes, rows, width,
    xs, nrm, fa, fb, ca, cb, qa, qb, dp, dpg, dwo, dgm, dbm, act_hbm, w_in_hbm, gain_in_ref,
    d_pair_ref, dw_in_ref, dw_out_ref, dgain_in_ref, dbias_in_ref, dgain_mid_ref, dbias_mid_ref,
    dpr, dxs, act_ref, w_in_ref, in_sem,
):
    pairs = rows * width
    hid, chan = fa.shape[1], nrm.shape[1]
    scale = 1.0 / width
    loads = [
        pltpu.make_async_copy(w_in_hbm, w_in_ref, in_sem.at[0]),
        pltpu.make_async_copy(act_hbm, act_ref, in_sem.at[1]),
    ]
    for load in loads:
        load.start()
    me = flat_slot(sizes, lax.axis_index("blk"), lax.axis_index("ch"), lax.axis_index("sub"))
    dw_out_ref[...] = dwo[...]
    dgain_mid_ref[...] = dgm[...]
    dbias_mid_ref[...] = dbm[...]
    for load in loads:
        load.wait()
    block = 8
    big = block * width

    def back(kb, sums):
        dgain, dbias = sums
        base = kb * block
        here = pl.ds(pl.multiple_of(base * width, big), big)
        left = outer_sum(
            width,
            lambda p, j: fb[pl.ds((base + p) * width + j, 1), :],
            lambda j: dp[pl.ds(j, width, stride=width), :],
            width, hid, block,
        )
        grad = jnp.concatenate(left, axis=0).astype(jnp.bfloat16).astype(jnp.float32)
        dpr[here, :hid] = (grad * qa[here, :]).astype(jnp.bfloat16)
        dpr[here, hid : 2 * hid] = (grad * ca[here, :]).astype(jnp.bfloat16)
        right = outer_sum(
            width,
            lambda p, i: fa[pl.ds((base + p) * width + i, 1), :],
            lambda i: dp[pl.ds(pl.multiple_of(i * width, width), width), :],
            width, hid, block,
        )
        grad = jnp.concatenate(right, axis=0).astype(jnp.bfloat16).astype(jnp.float32)
        dpr[here, 2 * hid : 3 * hid] = (grad * qb[here, :]).astype(jnp.bfloat16)
        dpr[here, 3 * hid : 4 * hid] = (grad * cb[here, :]).astype(jnp.bfloat16)
        dpr[here, 4 * hid :] = dpg[here, :]
        d_x = dot_t(dpr[here, :], w_in_ref[...])
        dxs[here, :] = d_x
        dgain = dgain + jnp.sum(d_x * nrm[here, :], axis=0, keepdims=True)
        dbias = dbias + jnp.sum(d_x, axis=0, keepdims=True)
        return dgain, dbias

    none = jnp.zeros((1, chan), jnp.float32)
    dgain, dbias = lax.fori_loop(0, width // block, back, (none, none))
    dgain_in_ref[...] = dgain * scale
    dbias_in_ref[...] = dbias * scale
    dw_in_ref[...] = t_dot(xs[...], dpr[...]) * scale
    _, inverse = norm_rows(act_ref[...].astype(jnp.float32))
    own = pl.ds(pl.multiple_of(me * pairs, pairs), pairs)
    normed = nrm[own, :]
    v = dxs[own, :] * gain_in_ref[...]
    d_pair_ref[...] = (inverse * (v - lane_mean(v) - normed * lane_mean(v * normed))).astype(
        jnp.bfloat16
    )


def fused(sizes, pair_act, pair_grad, pair_mask, w_in, w_out, gain_in, bias_in, gain_mid, bias_mid):
    rows, width, chan = pair_act.shape
    hid = w_out.shape[0]
    pairs = rows * width
    chips = sizes[0] * sizes[1]
    slots = chips * sizes[2]
    full = slots * pairs
    f32, low = jnp.float32, jnp.bfloat16
    vmem = pl.BlockSpec(memory_space=pltpu.VMEM)
    hbm = pl.BlockSpec(memory_space=pltpu.HBM)
    act = pair_act.reshape(pairs, chan)
    gain_row = gain_in.reshape(1, chan)
    vector = jax.ShapeDtypeStruct((1, hid), f32)
    big = jax.ShapeDtypeStruct((full, hid), f32)
    big_low = jax.ShapeDtypeStruct((full, hid), low)
    kept = pl.pallas_call(
        functools.partial(front_kernel, sizes, rows, width),
        out_shape=(big_low,) + (big,) * 8 + (big_low, jax.ShapeDtypeStruct(w_out.shape, f32), vector, vector),
        in_specs=[hbm] * 5 + [vmem] * 4,
        out_specs=(vmem,) * 13,
        scratch_shapes=[
            pltpu.VMEM((slots, pairs + PAD, chan), low),
            pltpu.VMEM((slots, pairs, chan), low),
            pltpu.VMEM((rows, width), jnp.int32),
            pltpu.VMEM(w_in.shape, low),
            pltpu.VMEM(w_out.shape, low),
            pltpu.VMEM((full, chan), f32),
            pltpu.VMEM((full, hid), low),
            pltpu.VMEM((full, chan), low),
            pltpu.SemaphoreType.DMA((5,)),
            pltpu.SemaphoreType.DMA((2, chips)),
            pltpu.SemaphoreType.DMA((2, slots)),
            pltpu.SemaphoreType.DMA((2, slots)),
        ],
        compiler_params=pltpu.CompilerParams(
            collective_id=0, has_side_effects=True, vmem_limit_bytes=VMEM_BYTES
        ),
    )(
        act, pair_grad.reshape(pairs, chan), pair_mask, w_in, w_out, gain_row,
        bias_in.reshape(1, chan), gain_mid.reshape(1, hid), bias_mid.reshape(1, hid),
    )
    out = pl.pallas_call(
        functools.partial(back_kernel, sizes, rows, width),
        out_shape=(
            jax.ShapeDtypeStruct((pairs, chan), low),
            jax.ShapeDtypeStruct(w_in.shape, f32),
            jax.ShapeDtypeStruct(w_out.shape, f32),
        ) + (vector,) * 4,
        in_specs=[vmem] * 13 + [hbm, hbm, vmem],
        out_specs=(vmem,) * 7,
        scratch_shapes=[
            pltpu.VMEM((full, w_in.shape[1]), low),
            pltpu.VMEM((full, chan), f32),
            pltpu.VMEM((pairs, chan), low),
            pltpu.VMEM(w_in.shape, low),
            pltpu.SemaphoreType.DMA((2,)),
        ],
        compiler_params=pltpu.CompilerParams(vmem_limit_bytes=VMEM_BYTES),
    )(*kept, act, w_in, gain_row)
    return (out[0].reshape(rows, width, chan), out[1], out[2]) + tuple(
        piece.reshape(-1) for piece in out[3:]
    )


def choose(mesh, *args):
    rows, width, chan = args[0].shape
    sizes = (mesh.shape["blk"], mesh.shape["ch"], mesh.shape["sub"])
    fits = width * width * chan * 128 <= VMEM_BYTES
    whole = width % 32 == 0 and 8 % rows == 0 and chan >= width and chan == 128 and args[4].shape[0] == 128
    if fits and whole and rows * sizes[0] * sizes[1] * sizes[2] == width:
        return fused(sizes, *args)
    return shards(*args)


def solution(mesh):
    in_specs = (
        P(("grp", "blk", "ch", "sub"), None, None),
        P(("grp", "blk", "ch", "sub"), None, None),
        P(("grp", "blk", "ch", "sub"), None),
        P(),
        P(),
        P(),
        P(),
        P(),
        P(),
    )
    out_specs = (
        P(("grp", "blk", "ch", "sub"), None, None),
        P("grp", None),
        P("grp", None),
        P("grp"),
        P("grp"),
        P("grp"),
        P("grp"),
    )
    body = functools.partial(choose, mesh)
    return jax.shard_map(body, mesh=mesh, in_specs=in_specs, out_specs=out_specs, check_vma=False)
```

```python
import functools

import jax
import jax.numpy as jnp
from jax import lax
from jax.experimental import pallas as pl
from jax.experimental.pallas import tpu as pltpu
from jax.sharding import PartitionSpec as P


def norm_parts(values):
    center = values - jnp.mean(values, axis=-1, keepdims=True)
    inverse = lax.rsqrt(jnp.mean(center * center, axis=-1, keepdims=True) + 1e-05)
    return (center * inverse, inverse)


def norm_back(upstream, normed, inverse):
    first = jnp.mean(upstream, axis=-1, keepdims=True)
    second = jnp.mean(upstream * normed, axis=-1, keepdims=True)
    return inverse * (upstream - first - normed * second)


def shards(pair_act, pair_grad, pair_mask, w_in, w_out, gain_in, bias_in, gain_mid, bias_mid):
    rows, width, chan = pair_act.shape
    hidden = w_out.shape[0]
    normed, inverse = norm_parts(pair_act.astype(jnp.float32))
    x_low = (normed * gain_in + bias_in).astype(jnp.bfloat16)
    flat_x = x_low.reshape(rows * width, chan)
    proj = jnp.dot(flat_x, w_in, preferred_element_type=jnp.float32).reshape(rows, width, -1)
    maskf = pair_mask.astype(jnp.float32)[:, :, None]
    sig_a = jax.nn.sigmoid(proj[..., :hidden])
    val_a = proj[..., hidden : 2 * hidden]
    sig_b = jax.nn.sigmoid(proj[..., 2 * hidden : 3 * hidden])
    val_b = proj[..., 3 * hidden : 4 * hidden]
    sig_g = jax.nn.sigmoid(proj[..., 4 * hidden :])
    fac_a = (maskf * sig_a * val_a).astype(jnp.bfloat16)
    fac_b = (maskf * sig_b * val_b).astype(jnp.bfloat16)
    stacked = jnp.transpose(jnp.stack([fac_a, fac_b]), (0, 3, 1, 2))
    grouped = lax.all_to_all(stacked, ("ch", "sub"), split_axis=1, concat_axis=2, tiled=True)
    left_loc = grouped[0]
    right_loc = grouped[1]
    stripe = left_loc.shape[1]
    own_start = lax.axis_index("blk") * stripe
    columns = lax.dynamic_slice_in_dim(
        lax.all_gather(left_loc, "blk", axis=1, tiled=True), own_start, stripe, 2
    )
    total = jnp.einsum(
        "hki,hkj->hij",
        columns,
        lax.all_gather(right_loc, "blk", axis=1, tiled=True),
        preferred_element_type=jnp.float32,
    )
    returned_prod = lax.all_to_all(
        total.astype(jnp.bfloat16), ("ch", "sub"), split_axis=1, concat_axis=0, tiled=True
    )
    prod = jnp.transpose(returned_prod, (1, 2, 0)).astype(jnp.float32)
    mid, inverse_mid = norm_parts(prod)
    y_low = (mid * gain_mid + bias_mid).astype(jnp.bfloat16)
    flat_y = y_low.reshape(rows * width, hidden)
    outp = jnp.dot(flat_y, w_out, preferred_element_type=jnp.float32).reshape(rows, width, chan)
    upstream = pair_grad.astype(jnp.float32)
    d_out = (upstream * sig_g).astype(jnp.bfloat16)
    d_sig = upstream * outp
    flat_d = d_out.reshape(rows * width, chan)
    dw_out_part = jnp.dot(flat_y.T, flat_d, preferred_element_type=jnp.float32)
    d_mid = jnp.dot(flat_d, w_out.T, preferred_element_type=jnp.float32).reshape(
        rows, width, hidden
    )
    dgain_mid_part = jnp.sum(d_mid * mid, axis=(0, 1))
    dbias_mid_part = jnp.sum(d_mid, axis=(0, 1))
    mid_totals = lax.psum((dw_out_part, dgain_mid_part, dbias_mid_part), ("blk", "ch", "sub"))
    d_prod = norm_back(d_mid * gain_mid, mid, inverse_mid).astype(jnp.bfloat16)
    d_groups = lax.all_to_all(
        jnp.transpose(d_prod, (2, 0, 1)), ("ch", "sub"), split_axis=0, concat_axis=1, tiled=True
    )
    piece = lax.all_gather(d_groups, "blk", axis=1, tiled=True)
    part_left = jnp.einsum("hkj,hij->hki", right_loc, piece, preferred_element_type=jnp.float32)
    grad_left = part_left
    grad_right = jnp.einsum("hki,hij->hkj", left_loc, piece, preferred_element_type=jnp.float32)
    grad_left, grad_right = (grad_left, grad_right)
    both_grads = jnp.stack([grad_left, grad_right]).astype(jnp.bfloat16)
    returned_grads = lax.all_to_all(
        both_grads, ("ch", "sub"), split_axis=2, concat_axis=1, tiled=True
    )
    pair_grads = jnp.transpose(returned_grads, (0, 2, 3, 1)).astype(jnp.float32)
    grad_a = pair_grads[0]
    grad_b = pair_grads[1]
    d_gate_a = grad_a * maskf * val_a * sig_a * (1.0 - sig_a)
    d_val_a = grad_a * maskf * sig_a
    d_gate_b = grad_b * maskf * val_b * sig_b * (1.0 - sig_b)
    d_val_b = grad_b * maskf * sig_b
    d_gate_g = d_sig * sig_g * (1.0 - sig_g)
    d_proj = jnp.concatenate([d_gate_a, d_val_a, d_gate_b, d_val_b, d_gate_g], axis=-1).astype(
        jnp.bfloat16
    )
    flat_p = d_proj.reshape(rows * width, -1)
    dw_in_part = jnp.dot(flat_x.T, flat_p, preferred_element_type=jnp.float32)
    d_x = jnp.dot(flat_p, w_in.T, preferred_element_type=jnp.float32).reshape(rows, width, chan)
    dgain_in_part = jnp.sum(d_x * normed, axis=(0, 1))
    dbias_in_part = jnp.sum(d_x, axis=(0, 1))
    d_pair = norm_back(d_x * gain_in, normed, inverse).astype(jnp.bfloat16)
    scale = 1.0 / width
    in_totals = lax.psum((dw_in_part, dgain_in_part, dbias_in_part), ("blk", "ch", "sub"))
    sums = (in_totals[0], in_totals[1], in_totals[2], mid_totals[0], mid_totals[1], mid_totals[2])
    return (
        d_pair,
        sums[0] * scale,
        sums[3] * scale,
        sums[1] * scale,
        sums[2] * scale,
        sums[4] * scale,
        sums[5] * scale,
    )


MESH = pl.DeviceIdType.MESH
PAD = 16
VMEM_BYTES = 58 * 1024 * 1024


def flat_slot(sizes, blk, ch, sub):
    return (blk * sizes[1] + ch) * sizes[2] + sub


def lane_mean(values):
    return jnp.mean(values, axis=-1, keepdims=True)


def norm_rows(values):
    center = values - lane_mean(values)
    inverse = lax.rsqrt(lane_mean(center * center) + 1e-05)
    return center * inverse, inverse


def sigm(values):
    return 0.5 * jnp.tanh(0.5 * values) + 0.5


def dot_t(left, right):
    return lax.dot_general(left, right, (((1,), (1,)), ((), ())), preferred_element_type=jnp.float32)


def t_dot(left, right):
    return lax.dot_general(left, right, (((0,), (0,)), ((), ())), preferred_element_type=jnp.float32)


def outer_sum(length, row_of, vec_of, width, chan, block):
    step = 4

    def body(t, acc):
        acc = list(acc)
        for s in range(step):
            q = t * step + s
            vec = vec_of(q)
            for p in range(block):
                acc[p] = acc[p] + row_of(p, q) * vec
        return tuple(acc)

    zero = jnp.zeros((width, chan), jnp.float32)
    return lax.fori_loop(0, length // step, body, (zero,) * block)


def front_kernel(
    sizes, rows, width,
    act_hbm, grad_hbm, mask_hbm, w_in_hbm, w_out_hbm, vec_hbm,
    xs, nrm, fa, fb, ca, cb, qa, qb, dp, dpg, dw_out_ref, dgain_mid_ref, dbias_mid_ref,
    ga, gg, mask_ref, w_in_ref, w_out_ref, vec_refs, sg, ys, dos, in_sem, send_sem, recv_sem, core_send,
):
    nz, nx, nc = sizes
    chips = nz * nx
    pairs = rows * width
    chan = w_out_ref.shape[1]
    hid = w_out_ref.shape[0]
    scale = 1.0 / width
    z, x, c = lax.axis_index("blk"), lax.axis_index("ch"), lax.axis_index("sub")
    y = lax.axis_index("grp")
    me = flat_slot(sizes, z, x, c)
    barrier = pltpu.get_barrier_semaphore()
    others = [
        (lax.rem(z + s, nz), lax.rem(x + r, nx))
        for r in range(nx) for s in range(nz) if s or r
    ]
    peers = [(y, zz, xx, c) for zz, xx in others]
    cores = [(y, z, x, lax.rem(c + s, nc)) for s in range(1, nc)]
    for peer in peers + cores:
        pl.semaphore_signal(barrier, inc=1, device_id=peer, device_id_type=MESH)
    loads = [
        pltpu.make_async_copy(act_hbm, ga.at[me, pl.ds(0, pairs)], in_sem.at[0]),
        pltpu.make_async_copy(mask_hbm, mask_ref, in_sem.at[1]),
        pltpu.make_async_copy(grad_hbm, gg.at[me], in_sem.at[2]),
        pltpu.make_async_copy(w_in_hbm, w_in_ref, in_sem.at[3]),
        pltpu.make_async_copy(w_out_hbm, w_out_ref, in_sem.at[4]),
    ] + [
        pltpu.make_async_copy(src, dst, in_sem.at[5 + n])
        for n, (src, dst) in enumerate(zip(vec_hbm, vec_refs))
    ]
    for load in loads:
        load.start()
    loads[1].wait()
    ga[me, pairs:, :] = jnp.zeros((PAD, chan), jnp.bfloat16)
    mine = mask_ref[...].astype(jnp.float32)
    ga[me, pairs:, :width] = jnp.concatenate(
        [jnp.broadcast_to(mine[r : r + 1, :], (PAD // rows, width)) for r in range(rows)], axis=0
    ).astype(jnp.bfloat16)
    loads[0].wait()
    pl.semaphore_wait(barrier, len(peers) + len(cores))

    bufs = (ga, gg)

    def chip_copy(which, slot, n, peer):
        return pltpu.make_async_remote_copy(
            src_ref=bufs[which].at[slot], dst_ref=bufs[which].at[slot],
            send_sem=send_sem.at[which, n], recv_sem=recv_sem.at[which, slot],
            device_id=peer, device_id_type=MESH,
        )

    def core_copy(which, slot, n):
        return pltpu.make_async_remote_copy(
            src_ref=bufs[which].at[slot], dst_ref=bufs[which].at[slot],
            send_sem=core_send.at[which, n], recv_sem=recv_sem.at[which, slot],
            device_id=cores[n // chips], device_id_type=MESH,
        )

    def send_own(which):
        for n, peer in enumerate(peers):
            chip_copy(which, me, n, peer).start()
        for k in range(nc - 1):
            core_copy(which, me, k * chips).start()

    def take(which, n):
        zz, xx = others[n - 1]
        slot = flat_slot(sizes, zz, xx, c)
        chip_copy(which, slot, 0, peers[0]).wait_recv()
        for k in range(nc - 1):
            core_copy(which, slot, k * chips + n).start()

    def take_core(which, slot):
        chip_copy(which, slot, 0, peers[0]).wait_recv()

    send_own(0)
    for load in loads[5:]:
        load.wait()
    gain_in, bias_in, gain_mid, bias_mid = [ref[...] for ref in vec_refs]
    at_row = lax.broadcasted_iota(jnp.int32, (width, chan), 0)
    at_lane = lax.broadcasted_iota(jnp.int32, (width, chan), 1)
    on_diag = at_row == at_lane
    ones = jnp.ones((chan, chan), jnp.bfloat16)

    def project(slots):
        act = jnp.concatenate([ga[s, :pairs, :] for s in slots], axis=0)
        lines = [ga[s, pairs:, :].astype(jnp.float32) for s in slots]
        diag = [
            jnp.where(on_diag, jnp.broadcast_to(line[r * (PAD // rows)][None, :], (width, chan)), 0.0)
            for line in lines for r in range(rows)
        ]
        mask = jnp.dot(
            jnp.concatenate(diag, axis=0).astype(jnp.bfloat16), ones,
            preferred_element_type=jnp.float32,
        )
        normed, _ = norm_rows(act.astype(jnp.float32))
        x_low = (normed * gain_in + bias_in).astype(jnp.bfloat16)

        def put(ref, value):
            for p, s in enumerate(slots):
                ref[pl.ds(pl.multiple_of(s * pairs, pairs), pairs), :] = value[
                    p * pairs : (p + 1) * pairs
                ]

        put(nrm, normed)
        put(xs, x_low)
        proj = jnp.dot(x_low, w_in_ref[...], preferred_element_type=jnp.float32)
        for at, fac, coef, gate in ((0, fa, ca, qa), (2, fb, cb, qb)):
            sig = sigm(proj[:, at * hid : (at + 1) * hid])
            val = proj[:, (at + 1) * hid : (at + 2) * hid]
            masked = mask * sig
            full = masked * val
            put(fac, full.astype(jnp.bfloat16).astype(jnp.float32))
            put(coef, masked)
            put(gate, full * (1.0 - sig))
        put(sg, sigm(proj[:, 4 * hid :]))

    loads[3].wait()
    loads[2].wait()
    for n in range(1, nz):
        take(0, n)
    send_own(1)
    for r in range(nx):
        if r:
            for n in range(r * nz, (r + 1) * nz):
                take(0, n)
        xx = lax.rem(x + r, nx)
        project([flat_slot(sizes, lax.rem(z + s, nz), xx, c) for s in range(nz)])
    for k in range(1, nc):
        cc = lax.rem(c + k, nc)
        for r in range(nx):
            xx = lax.rem(x + r, nx)
            slots = [flat_slot(sizes, lax.rem(z + s, nz), xx, cc) for s in range(nz)]
            for slot in slots:
                take_core(0, slot)
            project(slots)
    for n in range(1, chips):
        take(1, n)
    loads[4].wait()

    block = 8
    big = block * width

    def product(ib, carry):
        base = ib * block
        total = outer_sum(
            width,
            lambda p, k: fa[pl.ds(k * width + base + p, 1), :],
            lambda k: fb[pl.ds(pl.multiple_of(k * width, width), width), :],
            width, hid, block,
        )
        dp[pl.ds(pl.multiple_of(base * width, big), big), :] = jnp.concatenate(total, axis=0)
        return carry

    lax.fori_loop(0, width // block, product, 0)
    for k in range(1, nc):
        cc = lax.rem(c + k, nc)
        for zz, xx in [(z, x)] + others:
            take_core(1, flat_slot(sizes, zz, xx, cc))

    def middle(ib, sums):
        dgain, dbias = sums
        here = pl.ds(pl.multiple_of(ib * big, big), big)
        prod = dp[here, :].astype(jnp.bfloat16).astype(jnp.float32)
        mid, inverse = norm_rows(prod)
        y_low = (mid * gain_mid + bias_mid).astype(jnp.bfloat16)
        ys[here, :] = y_low
        per_block = block // rows
        upstream = jnp.concatenate(
            [gg[ib * per_block + s] for s in range(per_block)], axis=0
        ).astype(jnp.float32)
        sig = sg[here, :]
        outp = jnp.dot(y_low, w_out_ref[...], preferred_element_type=jnp.float32)
        d_out = (upstream * sig).astype(jnp.bfloat16)
        dos[here, :] = d_out
        dpg[here, :] = (upstream * outp * sig * (1.0 - sig)).astype(jnp.bfloat16)
        d_mid = dot_t(d_out, w_out_ref[...])
        dgain = dgain + jnp.sum(d_mid * mid, axis=0, keepdims=True)
        dbias = dbias + jnp.sum(d_mid, axis=0, keepdims=True)
        u = d_mid * gain_mid
        d_prod = inverse * (u - lane_mean(u) - mid * lane_mean(u * mid))
        dp[here, :] = d_prod.astype(jnp.bfloat16).astype(jnp.float32)
        return dgain, dbias

    none = jnp.zeros((1, hid), jnp.float32)
    dgain, dbias = lax.fori_loop(0, width // block, middle, (none, none))
    dgain_mid_ref[...] = dgain * scale
    dbias_mid_ref[...] = dbias * scale
    dw_out_ref[...] = t_dot(ys[...], dos[...]) * scale
    for which in (0, 1):
        for n, peer in enumerate(peers):
            chip_copy(which, me, n, peer).wait_send()
        for n in range((nc - 1) * chips):
            core_copy(which, me, n).wait_send()


def back_part(
    sizes, rows, width, xs, nrm, fa, fb, ca, cb, qa, qb, dp, dpg, ga, w_in_ref, gain_in_ref,
    d_pair_ref, dw_in_ref, dgain_in_ref, dbias_in_ref, dpr, dxs,
):
    pairs = rows * width
    hid, chan = fa.shape[1], nrm.shape[1]
    scale = 1.0 / width
    me = flat_slot(sizes, lax.axis_index("blk"), lax.axis_index("ch"), lax.axis_index("sub"))
    block = 8
    big = block * width

    def back(kb, sums):
        dgain, dbias = sums
        base = kb * block
        here = pl.ds(pl.multiple_of(base * width, big), big)
        left = outer_sum(
            width,
            lambda p, j: fb[pl.ds((base + p) * width + j, 1), :],
            lambda j: dp[pl.ds(j, width, stride=width), :],
            width, hid, block,
        )
        grad = jnp.concatenate(left, axis=0).astype(jnp.bfloat16).astype(jnp.float32)
        dpr[here, :hid] = (grad * qa[here, :]).astype(jnp.bfloat16)
        dpr[here, hid : 2 * hid] = (grad * ca[here, :]).astype(jnp.bfloat16)
        right = outer_sum(
            width,
            lambda p, i: fa[pl.ds((base + p) * width + i, 1), :],
            lambda i: dp[pl.ds(pl.multiple_of(i * width, width), width), :],
            width, hid, block,
        )
        grad = jnp.concatenate(right, axis=0).astype(jnp.bfloat16).astype(jnp.float32)
        dpr[here, 2 * hid : 3 * hid] = (grad * qb[here, :]).astype(jnp.bfloat16)
        dpr[here, 3 * hid : 4 * hid] = (grad * cb[here, :]).astype(jnp.bfloat16)
        dpr[here, 4 * hid :] = dpg[here, :]
        d_x = dot_t(dpr[here, :], w_in_ref[...])
        dxs[here, :] = d_x
        dgain = dgain + jnp.sum(d_x * nrm[here, :], axis=0, keepdims=True)
        dbias = dbias + jnp.sum(d_x, axis=0, keepdims=True)
        return dgain, dbias

    none = jnp.zeros((1, chan), jnp.float32)
    dgain, dbias = lax.fori_loop(0, width // block, back, (none, none))
    dgain_in_ref[...] = dgain * scale
    dbias_in_ref[...] = dbias * scale
    dw_in_ref[...] = t_dot(xs[...], dpr[...]) * scale
    _, inverse = norm_rows(ga[me, :pairs, :].astype(jnp.float32))
    own = pl.ds(pl.multiple_of(me * pairs, pairs), pairs)
    normed = nrm[own, :]
    v = dxs[own, :] * gain_in_ref[...]
    d_pair_ref[...] = (inverse * (v - lane_mean(v) - normed * lane_mean(v * normed))).astype(
        jnp.bfloat16
    )


def whole_kernel(
    sizes, rows, width,
    act_hbm, grad_hbm, mask_hbm, w_in_hbm, w_out_hbm, gain_in_hbm, bias_in_hbm, gain_mid_hbm, bias_mid_hbm,
    d_pair_ref, dw_in_ref, dw_out_ref, dgain_in_ref, dbias_in_ref, dgain_mid_ref, dbias_mid_ref,
    xs, nrm, fa, fb, ca, cb, qa, qb, dp, dpg, dpr, dxs,
    ga, gg, mask_ref, w_in_ref, w_out_ref, gain_in_ref, bias_in_ref, gain_mid_ref, bias_mid_ref,
    sg, ys, dos, in_sem, send_sem, recv_sem, core_send,
):
    front_kernel(
        sizes, rows, width, act_hbm, grad_hbm, mask_hbm, w_in_hbm, w_out_hbm,
        (gain_in_hbm, bias_in_hbm, gain_mid_hbm, bias_mid_hbm),
        xs, nrm, fa, fb, ca, cb, qa, qb, dp, dpg, dw_out_ref, dgain_mid_ref, dbias_mid_ref,
        ga, gg, mask_ref, w_in_ref, w_out_ref,
        (gain_in_ref, bias_in_ref, gain_mid_ref, bias_mid_ref),
        sg, ys, dos, in_sem, send_sem, recv_sem, core_send,
    )
    back_part(
        sizes, rows, width, xs, nrm, fa, fb, ca, cb, qa, qb, dp, dpg, ga, w_in_ref, gain_in_ref,
        d_pair_ref, dw_in_ref, dgain_in_ref, dbias_in_ref, dpr, dxs,
    )


def finish_kernel(count, *refs):
    sems = refs[-1]
    loads = [
        pltpu.make_async_copy(refs[n], refs[2 * count + n], sems.at[0, n]) for n in range(count)
    ]
    stores = [
        pltpu.make_async_copy(refs[2 * count + n], refs[count + n], sems.at[1, n])
        for n in range(count)
    ]
    for load in loads:
        load.start()
    for load, store in zip(loads, stores):
        load.wait()
        store.start()
    for store in stores:
        store.wait()


def fused(sizes, pair_act, pair_grad, pair_mask, w_in, w_out, gain_in, bias_in, gain_mid, bias_mid):
    rows, width, chan = pair_act.shape
    hid = w_out.shape[0]
    pairs = rows * width
    chips = sizes[0] * sizes[1]
    slots = chips * sizes[2]
    full = slots * pairs
    f32, low = jnp.float32, jnp.bfloat16
    vmem = pl.BlockSpec(memory_space=pltpu.VMEM)
    hbm = pl.BlockSpec(memory_space=pltpu.HBM)
    vector = jax.ShapeDtypeStruct((1, hid), f32)
    out = pl.pallas_call(
        functools.partial(whole_kernel, sizes, rows, width),
        out_shape=(
            jax.ShapeDtypeStruct((pairs, chan), low),
            jax.ShapeDtypeStruct(w_in.shape, f32),
            jax.ShapeDtypeStruct(w_out.shape, f32),
        ) + (vector,) * 4,
        in_specs=[hbm] * 9,
        out_specs=(vmem,) * 7,
        scratch_shapes=[pltpu.VMEM((full, chan), low)]
        + [pltpu.VMEM((full, hid), f32)] * 8
        + [
            pltpu.VMEM((full, hid), low),
            pltpu.VMEM((full, w_in.shape[1]), low),
            pltpu.VMEM((full, chan), f32),
            pltpu.VMEM((slots, pairs + PAD, chan), low),
            pltpu.VMEM((slots, pairs, chan), low),
            pltpu.VMEM((rows, width), jnp.int32),
            pltpu.VMEM(w_in.shape, low),
            pltpu.VMEM(w_out.shape, low),
        ]
        + [pltpu.VMEM((1, chan), f32)] * 4
        + [
            pltpu.VMEM((full, chan), f32),
            pltpu.VMEM((full, hid), low),
            pltpu.VMEM((full, chan), low),
            pltpu.SemaphoreType.DMA((9,)),
            pltpu.SemaphoreType.DMA((2, chips)),
            pltpu.SemaphoreType.DMA((2, slots)),
            pltpu.SemaphoreType.DMA((2, slots)),
        ],
        compiler_params=pltpu.CompilerParams(
            collective_id=0, has_side_effects=True, vmem_limit_bytes=VMEM_BYTES
        ),
    )(
        pair_act.reshape(pairs, chan), pair_grad.reshape(pairs, chan), pair_mask, w_in, w_out,
        gain_in.reshape(1, chan), bias_in.reshape(1, chan),
        gain_mid.reshape(1, hid), bias_mid.reshape(1, hid),
    )
    anywhere = pl.BlockSpec(memory_space=pl.ANY)
    out = pl.pallas_call(
        functools.partial(finish_kernel, len(out)),
        out_shape=tuple(jax.ShapeDtypeStruct(piece.shape, piece.dtype) for piece in out),
        in_specs=[anywhere] * len(out),
        out_specs=(anywhere,) * len(out),
        scratch_shapes=[pltpu.VMEM(piece.shape, piece.dtype) for piece in out]
        + [pltpu.SemaphoreType.DMA((2, len(out)))],
        compiler_params=pltpu.CompilerParams(vmem_limit_bytes=VMEM_BYTES),
    )(*out)
    return (out[0].reshape(rows, width, chan), out[1], out[2]) + tuple(
        piece.reshape(-1) for piece in out[3:]
    )


def choose(mesh, *args):
    rows, width, chan = args[0].shape
    sizes = (mesh.shape["blk"], mesh.shape["ch"], mesh.shape["sub"])
    fits = width * width * chan * 128 <= VMEM_BYTES
    whole = width % 32 == 0 and 8 % rows == 0 and chan >= width and chan == 128 and args[4].shape[0] == 128
    if fits and whole and rows * sizes[0] * sizes[1] * sizes[2] == width:
        return fused(sizes, *args)
    return shards(*args)


def solution(mesh):
    in_specs = (
        P(("grp", "blk", "ch", "sub"), None, None),
        P(("grp", "blk", "ch", "sub"), None, None),
        P(("grp", "blk", "ch", "sub"), None),
        P(),
        P(),
        P(),
        P(),
        P(),
        P(),
    )
    out_specs = (
        P(("grp", "blk", "ch", "sub"), None, None),
        P("grp", None),
        P("grp", None),
        P("grp"),
        P("grp"),
        P("grp"),
        P("grp"),
    )
    body = functools.partial(choose, mesh)
    return jax.shard_map(body, mesh=mesh, in_specs=in_specs, out_specs=out_specs, check_vma=False)
```

```python
import functools

import jax
import jax.numpy as jnp
from jax import lax
from jax.experimental import pallas as pl
from jax.experimental.pallas import tpu as pltpu
from jax.sharding import PartitionSpec as P


def norm_parts(values):
    center = values - jnp.mean(values, axis=-1, keepdims=True)
    inverse = lax.rsqrt(jnp.mean(center * center, axis=-1, keepdims=True) + 1e-05)
    return (center * inverse, inverse)


def norm_back(upstream, normed, inverse):
    first = jnp.mean(upstream, axis=-1, keepdims=True)
    second = jnp.mean(upstream * normed, axis=-1, keepdims=True)
    return inverse * (upstream - first - normed * second)


def shards(pair_act, pair_grad, pair_mask, w_in, w_out, gain_in, bias_in, gain_mid, bias_mid):
    rows, width, chan = pair_act.shape
    hidden = w_out.shape[0]
    normed, inverse = norm_parts(pair_act.astype(jnp.float32))
    x_low = (normed * gain_in + bias_in).astype(jnp.bfloat16)
    flat_x = x_low.reshape(rows * width, chan)
    proj = jnp.dot(flat_x, w_in, preferred_element_type=jnp.float32).reshape(rows, width, -1)
    maskf = pair_mask.astype(jnp.float32)[:, :, None]
    sig_a = jax.nn.sigmoid(proj[..., :hidden])
    val_a = proj[..., hidden : 2 * hidden]
    sig_b = jax.nn.sigmoid(proj[..., 2 * hidden : 3 * hidden])
    val_b = proj[..., 3 * hidden : 4 * hidden]
    sig_g = jax.nn.sigmoid(proj[..., 4 * hidden :])
    fac_a = (maskf * sig_a * val_a).astype(jnp.bfloat16)
    fac_b = (maskf * sig_b * val_b).astype(jnp.bfloat16)
    stacked = jnp.transpose(jnp.stack([fac_a, fac_b]), (0, 3, 1, 2))
    grouped = lax.all_to_all(stacked, ("ch", "sub"), split_axis=1, concat_axis=2, tiled=True)
    left_loc = grouped[0]
    right_loc = grouped[1]
    stripe = left_loc.shape[1]
    own_start = lax.axis_index("blk") * stripe
    columns = lax.dynamic_slice_in_dim(
        lax.all_gather(left_loc, "blk", axis=1, tiled=True), own_start, stripe, 2
    )
    total = jnp.einsum(
        "hki,hkj->hij",
        columns,
        lax.all_gather(right_loc, "blk", axis=1, tiled=True),
        preferred_element_type=jnp.float32,
    )
    returned_prod = lax.all_to_all(
        total.astype(jnp.bfloat16), ("ch", "sub"), split_axis=1, concat_axis=0, tiled=True
    )
    prod = jnp.transpose(returned_prod, (1, 2, 0)).astype(jnp.float32)
    mid, inverse_mid = norm_parts(prod)
    y_low = (mid * gain_mid + bias_mid).astype(jnp.bfloat16)
    flat_y = y_low.reshape(rows * width, hidden)
    outp = jnp.dot(flat_y, w_out, preferred_element_type=jnp.float32).reshape(rows, width, chan)
    upstream = pair_grad.astype(jnp.float32)
    d_out = (upstream * sig_g).astype(jnp.bfloat16)
    d_sig = upstream * outp
    flat_d = d_out.reshape(rows * width, chan)
    dw_out_part = jnp.dot(flat_y.T, flat_d, preferred_element_type=jnp.float32)
    d_mid = jnp.dot(flat_d, w_out.T, preferred_element_type=jnp.float32).reshape(
        rows, width, hidden
    )
    dgain_mid_part = jnp.sum(d_mid * mid, axis=(0, 1))
    dbias_mid_part = jnp.sum(d_mid, axis=(0, 1))
    mid_totals = lax.psum((dw_out_part, dgain_mid_part, dbias_mid_part), ("blk", "ch", "sub"))
    d_prod = norm_back(d_mid * gain_mid, mid, inverse_mid).astype(jnp.bfloat16)
    d_groups = lax.all_to_all(
        jnp.transpose(d_prod, (2, 0, 1)), ("ch", "sub"), split_axis=0, concat_axis=1, tiled=True
    )
    piece = lax.all_gather(d_groups, "blk", axis=1, tiled=True)
    part_left = jnp.einsum("hkj,hij->hki", right_loc, piece, preferred_element_type=jnp.float32)
    grad_left = part_left
    grad_right = jnp.einsum("hki,hij->hkj", left_loc, piece, preferred_element_type=jnp.float32)
    grad_left, grad_right = (grad_left, grad_right)
    both_grads = jnp.stack([grad_left, grad_right]).astype(jnp.bfloat16)
    returned_grads = lax.all_to_all(
        both_grads, ("ch", "sub"), split_axis=2, concat_axis=1, tiled=True
    )
    pair_grads = jnp.transpose(returned_grads, (0, 2, 3, 1)).astype(jnp.float32)
    grad_a = pair_grads[0]
    grad_b = pair_grads[1]
    d_gate_a = grad_a * maskf * val_a * sig_a * (1.0 - sig_a)
    d_val_a = grad_a * maskf * sig_a
    d_gate_b = grad_b * maskf * val_b * sig_b * (1.0 - sig_b)
    d_val_b = grad_b * maskf * sig_b
    d_gate_g = d_sig * sig_g * (1.0 - sig_g)
    d_proj = jnp.concatenate([d_gate_a, d_val_a, d_gate_b, d_val_b, d_gate_g], axis=-1).astype(
        jnp.bfloat16
    )
    flat_p = d_proj.reshape(rows * width, -1)
    dw_in_part = jnp.dot(flat_x.T, flat_p, preferred_element_type=jnp.float32)
    d_x = jnp.dot(flat_p, w_in.T, preferred_element_type=jnp.float32).reshape(rows, width, chan)
    dgain_in_part = jnp.sum(d_x * normed, axis=(0, 1))
    dbias_in_part = jnp.sum(d_x, axis=(0, 1))
    d_pair = norm_back(d_x * gain_in, normed, inverse).astype(jnp.bfloat16)
    scale = 1.0 / width
    in_totals = lax.psum((dw_in_part, dgain_in_part, dbias_in_part), ("blk", "ch", "sub"))
    sums = (in_totals[0], in_totals[1], in_totals[2], mid_totals[0], mid_totals[1], mid_totals[2])
    return (
        d_pair,
        sums[0] * scale,
        sums[3] * scale,
        sums[1] * scale,
        sums[2] * scale,
        sums[4] * scale,
        sums[5] * scale,
    )


MESH = pl.DeviceIdType.MESH
PAD = 16
VMEM_BYTES = 58 * 1024 * 1024


def flat_slot(sizes, blk, ch, sub):
    return (blk * sizes[1] + ch) * sizes[2] + sub


def lane_mean(values):
    return jnp.mean(values, axis=-1, keepdims=True)


def norm_rows(values):
    center = values - lane_mean(values)
    inverse = lax.rsqrt(lane_mean(center * center) + 1e-05)
    return center * inverse, inverse


def sigm(values):
    return 0.5 * jnp.tanh(0.5 * values) + 0.5


def dot_t(left, right):
    return lax.dot_general(left, right, (((1,), (1,)), ((), ())), preferred_element_type=jnp.float32)


def t_dot(left, right):
    return lax.dot_general(left, right, (((0,), (0,)), ((), ())), preferred_element_type=jnp.float32)


def outer_sum(length, row_of, vec_of, width, chan, block):
    step = 4

    def body(t, acc):
        acc = list(acc)
        for s in range(step):
            q = t * step + s
            vec = vec_of(q)
            for p in range(block):
                acc[p] = acc[p] + row_of(p, q) * vec
        return tuple(acc)

    zero = jnp.zeros((width, chan), jnp.float32)
    return lax.fori_loop(0, length // step, body, (zero,) * block)


def front_kernel(
    sizes, rows, width,
    act_hbm, grad_hbm, mask_hbm, w_in_hbm, w_out_hbm, vec_hbm,
    xs, nrm, fa, fb, ca, cb, qa, qb, dp, dpg, dw_out_ref, dgain_mid_ref, dbias_mid_ref,
    ga, gg, mask_ref, w_in_ref, w_out_ref, vec_refs, sg, ys, dos, in_sem, send_sem, recv_sem, core_send,
):
    nz, nx, nc = sizes
    chips = nz * nx
    pairs = rows * width
    chan = w_out_ref.shape[1]
    hid = w_out_ref.shape[0]
    scale = 1.0 / width
    z, x, c = lax.axis_index("blk"), lax.axis_index("ch"), lax.axis_index("sub")
    y = lax.axis_index("grp")
    me = flat_slot(sizes, z, x, c)
    barrier = pltpu.get_barrier_semaphore()
    others = [
        (lax.rem(z + s, nz), lax.rem(x + r, nx))
        for r in range(nx) for s in range(nz) if s or r
    ]
    peers = [(y, zz, xx, c) for zz, xx in others]
    cores = [(y, z, x, lax.rem(c + s, nc)) for s in range(1, nc)]
    for peer in peers + cores:
        pl.semaphore_signal(barrier, inc=1, device_id=peer, device_id_type=MESH)
    loads = [
        pltpu.make_async_copy(act_hbm, ga.at[me, pl.ds(0, pairs)], in_sem.at[0]),
        pltpu.make_async_copy(mask_hbm, mask_ref, in_sem.at[1]),
        pltpu.make_async_copy(grad_hbm, gg.at[me], in_sem.at[2]),
        pltpu.make_async_copy(w_in_hbm, w_in_ref, in_sem.at[3]),
        pltpu.make_async_copy(w_out_hbm, w_out_ref, in_sem.at[4]),
    ] + [
        pltpu.make_async_copy(src, dst, in_sem.at[5 + n])
        for n, (src, dst) in enumerate(zip(vec_hbm, vec_refs))
    ]
    for load in loads:
        load.start()
    loads[1].wait()
    ga[me, pairs:, :] = jnp.zeros((PAD, chan), jnp.bfloat16)
    mine = mask_ref[...].astype(jnp.float32)
    ga[me, pairs:, :width] = jnp.concatenate(
        [jnp.broadcast_to(mine[r : r + 1, :], (PAD // rows, width)) for r in range(rows)], axis=0
    ).astype(jnp.bfloat16)
    loads[0].wait()
    pl.semaphore_wait(barrier, len(peers) + len(cores))

    bufs = (ga, gg)

    def chip_copy(which, slot, n, peer):
        return pltpu.make_async_remote_copy(
            src_ref=bufs[which].at[slot], dst_ref=bufs[which].at[slot],
            send_sem=send_sem.at[which, n], recv_sem=recv_sem.at[which, slot],
            device_id=peer, device_id_type=MESH,
        )

    def core_copy(which, slot, n):
        return pltpu.make_async_remote_copy(
            src_ref=bufs[which].at[slot], dst_ref=bufs[which].at[slot],
            send_sem=core_send.at[which, n], recv_sem=recv_sem.at[which, slot],
            device_id=cores[n // chips], device_id_type=MESH,
        )

    def send_own(which):
        for n, peer in enumerate(peers):
            chip_copy(which, me, n, peer).start()
        for k in range(nc - 1):
            core_copy(which, me, k * chips).start()

    def take(which, n):
        zz, xx = others[n - 1]
        slot = flat_slot(sizes, zz, xx, c)
        chip_copy(which, slot, 0, peers[0]).wait_recv()
        for k in range(nc - 1):
            core_copy(which, slot, k * chips + n).start()

    def take_core(which, slot):
        chip_copy(which, slot, 0, peers[0]).wait_recv()

    send_own(0)
    for load in loads[5:]:
        load.wait()
    gain_in, bias_in, gain_mid, bias_mid = [ref[...] for ref in vec_refs]
    at_row = lax.broadcasted_iota(jnp.int32, (width, chan), 0)
    at_lane = lax.broadcasted_iota(jnp.int32, (width, chan), 1)
    on_diag = at_row == at_lane
    ones = jnp.ones((chan, chan), jnp.bfloat16)

    def project(slots):
        act = jnp.concatenate([ga[s, :pairs, :] for s in slots], axis=0)
        lines = [ga[s, pairs:, :].astype(jnp.float32) for s in slots]
        diag = [
            jnp.where(on_diag, jnp.broadcast_to(line[r * (PAD // rows)][None, :], (width, chan)), 0.0)
            for line in lines for r in range(rows)
        ]
        mask = jnp.dot(
            jnp.concatenate(diag, axis=0).astype(jnp.bfloat16), ones,
            preferred_element_type=jnp.float32,
        )
        normed, _ = norm_rows(act.astype(jnp.float32))
        x_low = (normed * gain_in + bias_in).astype(jnp.bfloat16)

        def put(ref, value):
            for p, s in enumerate(slots):
                ref[pl.ds(pl.multiple_of(s * pairs, pairs), pairs), :] = value[
                    p * pairs : (p + 1) * pairs
                ]

        put(nrm, normed)
        put(xs, x_low)
        proj = jnp.dot(x_low, w_in_ref[...], preferred_element_type=jnp.float32)
        for at, fac, coef, gate in ((0, fa, ca, qa), (2, fb, cb, qb)):
            sig = sigm(proj[:, at * hid : (at + 1) * hid])
            val = proj[:, (at + 1) * hid : (at + 2) * hid]
            masked = mask * sig
            full = masked * val
            put(fac, full.astype(jnp.bfloat16).astype(jnp.float32))
            put(coef, masked)
            put(gate, full * (1.0 - sig))
        put(sg, sigm(proj[:, 4 * hid :]))

    loads[3].wait()
    loads[2].wait()
    for n in range(1, nz):
        take(0, n)
    send_own(1)
    for r in range(nx):
        if r:
            for n in range(r * nz, (r + 1) * nz):
                take(0, n)
        xx = lax.rem(x + r, nx)
        project([flat_slot(sizes, lax.rem(z + s, nz), xx, c) for s in range(nz)])
    for k in range(1, nc):
        cc = lax.rem(c + k, nc)
        for r in range(nx):
            xx = lax.rem(x + r, nx)
            slots = [flat_slot(sizes, lax.rem(z + s, nz), xx, cc) for s in range(nz)]
            for slot in slots:
                take_core(0, slot)
            project(slots)
    for n in range(1, chips):
        take(1, n)
    loads[4].wait()

    block = 8
    big = block * width

    def product(ib, carry):
        base = ib * block
        total = outer_sum(
            width,
            lambda p, k: fa[pl.ds(k * width + base + p, 1), :],
            lambda k: fb[pl.ds(pl.multiple_of(k * width, width), width), :],
            width, hid, block,
        )
        dp[pl.ds(pl.multiple_of(base * width, big), big), :] = jnp.concatenate(total, axis=0)
        return carry

    lax.fori_loop(0, width // block, product, 0)
    for k in range(1, nc):
        cc = lax.rem(c + k, nc)
        for zz, xx in [(z, x)] + others:
            take_core(1, flat_slot(sizes, zz, xx, cc))

    def middle(ib, sums):
        dgain, dbias = sums
        here = pl.ds(pl.multiple_of(ib * big, big), big)
        prod = dp[here, :].astype(jnp.bfloat16).astype(jnp.float32)
        mid, inverse = norm_rows(prod)
        y_low = (mid * gain_mid + bias_mid).astype(jnp.bfloat16)
        ys[here, :] = y_low
        per_block = block // rows
        upstream = jnp.concatenate(
            [gg[ib * per_block + s] for s in range(per_block)], axis=0
        ).astype(jnp.float32)
        sig = sg[here, :]
        outp = jnp.dot(y_low, w_out_ref[...], preferred_element_type=jnp.float32)
        d_out = (upstream * sig).astype(jnp.bfloat16)
        dos[here, :] = d_out
        dpg[here, :] = (upstream * outp * sig * (1.0 - sig)).astype(jnp.bfloat16)
        d_mid = dot_t(d_out, w_out_ref[...])
        dgain = dgain + jnp.sum(d_mid * mid, axis=0, keepdims=True)
        dbias = dbias + jnp.sum(d_mid, axis=0, keepdims=True)
        u = d_mid * gain_mid
        d_prod = inverse * (u - lane_mean(u) - mid * lane_mean(u * mid))
        dp[here, :] = d_prod.astype(jnp.bfloat16).astype(jnp.float32)
        return dgain, dbias

    none = jnp.zeros((1, hid), jnp.float32)
    dgain, dbias = lax.fori_loop(0, width // block, middle, (none, none))
    dgain_mid_ref[...] = dgain * scale
    dbias_mid_ref[...] = dbias * scale
    dw_out_ref[...] = t_dot(ys[...], dos[...]) * scale
    for which in (0, 1):
        for n, peer in enumerate(peers):
            chip_copy(which, me, n, peer).wait_send()
        for n in range((nc - 1) * chips):
            core_copy(which, me, n).wait_send()


def back_part(
    sizes, rows, width, xs, nrm, fa, fb, ca, cb, qa, qb, dp, dpg, ga, w_in_ref, gain_in_ref,
    d_pair_ref, dw_in_ref, dgain_in_ref, dbias_in_ref, dpr, dxs,
    part_out, part_in, vec_out, vec_in, half_send, half_recv,
):
    nc = sizes[2]
    pairs = rows * width
    hid, chan = fa.shape[1], nrm.shape[1]
    scale = 1.0 / width
    z, x, c = lax.axis_index("blk"), lax.axis_index("ch"), lax.axis_index("sub")
    me = flat_slot(sizes, z, x, c)
    other = (lax.axis_index("grp"), z, x, lax.rem(c + 1, nc))
    block = 8
    big = block * width
    per_block = block // rows
    blocks = width // block // nc

    def slot_rows(n):
        return pl.ds(pl.multiple_of((n * nc + c) * pairs, pairs), pairs)

    def back(kb, sums):
        dgain, dbias = sums
        here = pl.ds(pl.multiple_of(kb * big, big), big)

        def pick(ref):
            return jnp.concatenate(
                [ref[slot_rows(kb * per_block + q), :] for q in range(per_block)], axis=0
            )

        def line(p):
            return ((kb * per_block + p // rows) * nc + c) * pairs + (p % rows) * width

        left = outer_sum(
            width,
            lambda p, j: fb[pl.ds(line(p) + j, 1), :],
            lambda j: dp[pl.ds(j, width, stride=width), :],
            width, hid, block,
        )
        grad = jnp.concatenate(left, axis=0).astype(jnp.bfloat16).astype(jnp.float32)
        dpr[here, :hid] = (grad * pick(qa)).astype(jnp.bfloat16)
        dpr[here, hid : 2 * hid] = (grad * pick(ca)).astype(jnp.bfloat16)
        right = outer_sum(
            width,
            lambda p, i: fa[pl.ds(line(p) + i, 1), :],
            lambda i: dp[pl.ds(pl.multiple_of(i * width, width), width), :],
            width, hid, block,
        )
        grad = jnp.concatenate(right, axis=0).astype(jnp.bfloat16).astype(jnp.float32)
        dpr[here, 2 * hid : 3 * hid] = (grad * pick(qb)).astype(jnp.bfloat16)
        dpr[here, 3 * hid : 4 * hid] = (grad * pick(cb)).astype(jnp.bfloat16)
        dpr[here, 4 * hid :] = pick(dpg)
        d_x = dot_t(dpr[here, :], w_in_ref[...])
        dxs[here, :] = d_x
        dgain = dgain + jnp.sum(d_x * pick(nrm), axis=0, keepdims=True)
        dbias = dbias + jnp.sum(d_x, axis=0, keepdims=True)
        return dgain, dbias

    none = jnp.zeros((1, chan), jnp.float32)
    dgain, dbias = lax.fori_loop(0, blocks, back, (none, none))
    vec_out[0:8, :] = jnp.broadcast_to(dgain, (8, chan))
    vec_out[8:16, :] = jnp.broadcast_to(dbias, (8, chan))
    x_half = jnp.concatenate([xs[slot_rows(n), :] for n in range(sizes[0] * sizes[1])], axis=0)
    part_out[...] = t_dot(x_half, dpr[...]).astype(jnp.bfloat16)
    swaps = [
        pltpu.make_async_remote_copy(
            src_ref=src, dst_ref=dst, send_sem=half_send.at[n], recv_sem=half_recv.at[n],
            device_id=other, device_id_type=MESH,
        )
        for n, (src, dst) in enumerate(((part_out, part_in), (vec_out, vec_in)))
    ]
    for swap in swaps:
        swap.start()
    _, inverse = norm_rows(ga[me, :pairs, :].astype(jnp.float32))
    own = pl.ds(pl.multiple_of(me * pairs, pairs), pairs)
    kept = pl.ds(pl.multiple_of(me // nc * pairs, pairs), pairs)
    normed = nrm[own, :]
    v = dxs[kept, :] * gain_in_ref[...]
    d_pair_ref[...] = (inverse * (v - lane_mean(v) - normed * lane_mean(v * normed))).astype(
        jnp.bfloat16
    )
    for swap in swaps:
        swap.wait()
    dw_in_ref[...] = (
        part_out[...].astype(jnp.float32) + part_in[...].astype(jnp.float32)
    ) * scale
    dgain_in_ref[...] = (vec_out[0:1, :] + vec_in[0:1, :]) * scale
    dbias_in_ref[...] = (vec_out[8:9, :] + vec_in[8:9, :]) * scale


def whole_kernel(
    sizes, rows, width,
    act_hbm, grad_hbm, mask_hbm, w_in_hbm, w_out_hbm, gain_in_hbm, bias_in_hbm, gain_mid_hbm, bias_mid_hbm,
    d_pair_ref, dw_in_ref, dw_out_ref, dgain_in_ref, dbias_in_ref, dgain_mid_ref, dbias_mid_ref,
    xs, nrm, fa, fb, ca, cb, qa, qb, dp, dpg, dpr, dxs,
    ga, gg, mask_ref, w_in_ref, w_out_ref, gain_in_ref, bias_in_ref, gain_mid_ref, bias_mid_ref,
    sg, ys, dos, in_sem, send_sem, recv_sem, core_send,
    part_out, part_in, vec_out, vec_in, half_send, half_recv,
):
    front_kernel(
        sizes, rows, width, act_hbm, grad_hbm, mask_hbm, w_in_hbm, w_out_hbm,
        (gain_in_hbm, bias_in_hbm, gain_mid_hbm, bias_mid_hbm),
        xs, nrm, fa, fb, ca, cb, qa, qb, dp, dpg, dw_out_ref, dgain_mid_ref, dbias_mid_ref,
        ga, gg, mask_ref, w_in_ref, w_out_ref,
        (gain_in_ref, bias_in_ref, gain_mid_ref, bias_mid_ref),
        sg, ys, dos, in_sem, send_sem, recv_sem, core_send,
    )
    back_part(
        sizes, rows, width, xs, nrm, fa, fb, ca, cb, qa, qb, dp, dpg, ga, w_in_ref, gain_in_ref,
        d_pair_ref, dw_in_ref, dgain_in_ref, dbias_in_ref, dpr, dxs,
        part_out, part_in, vec_out, vec_in, half_send, half_recv,
    )


def finish_kernel(count, *refs):
    sems = refs[-1]
    loads = [
        pltpu.make_async_copy(refs[n], refs[2 * count + n], sems.at[0, n]) for n in range(count)
    ]
    stores = [
        pltpu.make_async_copy(refs[2 * count + n], refs[count + n], sems.at[1, n])
        for n in range(count)
    ]
    for load in loads:
        load.start()
    for load, store in zip(loads, stores):
        load.wait()
        store.start()
    for store in stores:
        store.wait()


def fused(sizes, pair_act, pair_grad, pair_mask, w_in, w_out, gain_in, bias_in, gain_mid, bias_mid):
    rows, width, chan = pair_act.shape
    hid = w_out.shape[0]
    pairs = rows * width
    chips = sizes[0] * sizes[1]
    slots = chips * sizes[2]
    full = slots * pairs
    f32, low = jnp.float32, jnp.bfloat16
    vmem = pl.BlockSpec(memory_space=pltpu.VMEM)
    hbm = pl.BlockSpec(memory_space=pltpu.HBM)
    vector = jax.ShapeDtypeStruct((1, hid), f32)
    out = pl.pallas_call(
        functools.partial(whole_kernel, sizes, rows, width),
        out_shape=(
            jax.ShapeDtypeStruct((pairs, chan), low),
            jax.ShapeDtypeStruct(w_in.shape, f32),
            jax.ShapeDtypeStruct(w_out.shape, f32),
        ) + (vector,) * 4,
        in_specs=[hbm] * 9,
        out_specs=(vmem,) * 7,
        scratch_shapes=[pltpu.VMEM((full, chan), low)]
        + [pltpu.VMEM((full, hid), f32)] * 8
        + [
            pltpu.VMEM((full, hid), low),
            pltpu.VMEM((full // sizes[2], w_in.shape[1]), low),
            pltpu.VMEM((full // sizes[2], chan), f32),
            pltpu.VMEM((slots, pairs + PAD, chan), low),
            pltpu.VMEM((slots, pairs, chan), low),
            pltpu.VMEM((rows, width), jnp.int32),
            pltpu.VMEM(w_in.shape, low),
            pltpu.VMEM(w_out.shape, low),
        ]
        + [pltpu.VMEM((1, chan), f32)] * 4
        + [
            pltpu.VMEM((full, chan), f32),
            pltpu.VMEM((full, hid), low),
            pltpu.VMEM((full, chan), low),
            pltpu.SemaphoreType.DMA((9,)),
            pltpu.SemaphoreType.DMA((2, chips)),
            pltpu.SemaphoreType.DMA((2, slots)),
            pltpu.SemaphoreType.DMA((2, slots)),
            pltpu.VMEM(w_in.shape, low),
            pltpu.VMEM(w_in.shape, low),
            pltpu.VMEM((16, chan), f32),
            pltpu.VMEM((16, chan), f32),
            pltpu.SemaphoreType.DMA((2,)),
            pltpu.SemaphoreType.DMA((2,)),
        ],
        compiler_params=pltpu.CompilerParams(
            collective_id=0, has_side_effects=True, vmem_limit_bytes=VMEM_BYTES
        ),
    )(
        pair_act.reshape(pairs, chan), pair_grad.reshape(pairs, chan), pair_mask, w_in, w_out,
        gain_in.reshape(1, chan), bias_in.reshape(1, chan),
        gain_mid.reshape(1, hid), bias_mid.reshape(1, hid),
    )
    anywhere = pl.BlockSpec(memory_space=pl.ANY)
    out = pl.pallas_call(
        functools.partial(finish_kernel, len(out)),
        out_shape=tuple(jax.ShapeDtypeStruct(piece.shape, piece.dtype) for piece in out),
        in_specs=[anywhere] * len(out),
        out_specs=(anywhere,) * len(out),
        scratch_shapes=[pltpu.VMEM(piece.shape, piece.dtype) for piece in out]
        + [pltpu.SemaphoreType.DMA((2, len(out)))],
        compiler_params=pltpu.CompilerParams(vmem_limit_bytes=VMEM_BYTES),
    )(*out)
    return (out[0].reshape(rows, width, chan), out[1], out[2]) + tuple(
        piece.reshape(-1) for piece in out[3:]
    )


def choose(mesh, *args):
    rows, width, chan = args[0].shape
    sizes = (mesh.shape["blk"], mesh.shape["ch"], mesh.shape["sub"])
    fits = width * width * chan * 128 <= VMEM_BYTES
    whole = sizes[2] == 2 and width % 32 == 0 and 8 % rows == 0 and chan >= width and chan == 128 and args[4].shape[0] == 128
    if fits and whole and rows * sizes[0] * sizes[1] * sizes[2] == width:
        return fused(sizes, *args)
    return shards(*args)


def solution(mesh):
    in_specs = (
        P(("grp", "blk", "ch", "sub"), None, None),
        P(("grp", "blk", "ch", "sub"), None, None),
        P(("grp", "blk", "ch", "sub"), None),
        P(),
        P(),
        P(),
        P(),
        P(),
        P(),
    )
    out_specs = (
        P(("grp", "blk", "ch", "sub"), None, None),
        P("grp", None),
        P("grp", None),
        P("grp"),
        P("grp"),
        P("grp"),
        P("grp"),
    )
    body = functools.partial(choose, mesh)
    return jax.shard_map(body, mesh=mesh, in_specs=in_specs, out_specs=out_specs, check_vma=False)
```

```python
import functools

import jax
import jax.numpy as jnp
from jax import lax
from jax.experimental import pallas as pl
from jax.experimental.pallas import tpu as pltpu
from jax.sharding import PartitionSpec as P


def norm_parts(values):
    center = values - jnp.mean(values, axis=-1, keepdims=True)
    inverse = lax.rsqrt(jnp.mean(center * center, axis=-1, keepdims=True) + 1e-05)
    return (center * inverse, inverse)


def norm_back(upstream, normed, inverse):
    first = jnp.mean(upstream, axis=-1, keepdims=True)
    second = jnp.mean(upstream * normed, axis=-1, keepdims=True)
    return inverse * (upstream - first - normed * second)


def shards(pair_act, pair_grad, pair_mask, w_in, w_out, gain_in, bias_in, gain_mid, bias_mid):
    rows, width, chan = pair_act.shape
    hidden = w_out.shape[0]
    normed, inverse = norm_parts(pair_act.astype(jnp.float32))
    x_low = (normed * gain_in + bias_in).astype(jnp.bfloat16)
    flat_x = x_low.reshape(rows * width, chan)
    proj = jnp.dot(flat_x, w_in, preferred_element_type=jnp.float32).reshape(rows, width, -1)
    maskf = pair_mask.astype(jnp.float32)[:, :, None]
    sig_a = jax.nn.sigmoid(proj[..., :hidden])
    val_a = proj[..., hidden : 2 * hidden]
    sig_b = jax.nn.sigmoid(proj[..., 2 * hidden : 3 * hidden])
    val_b = proj[..., 3 * hidden : 4 * hidden]
    sig_g = jax.nn.sigmoid(proj[..., 4 * hidden :])
    fac_a = (maskf * sig_a * val_a).astype(jnp.bfloat16)
    fac_b = (maskf * sig_b * val_b).astype(jnp.bfloat16)
    stacked = jnp.transpose(jnp.stack([fac_a, fac_b]), (0, 3, 1, 2))
    grouped = lax.all_to_all(stacked, ("ch", "sub"), split_axis=1, concat_axis=2, tiled=True)
    left_loc = grouped[0]
    right_loc = grouped[1]
    stripe = left_loc.shape[1]
    own_start = lax.axis_index("blk") * stripe
    columns = lax.dynamic_slice_in_dim(
        lax.all_gather(left_loc, "blk", axis=1, tiled=True), own_start, stripe, 2
    )
    total = jnp.einsum(
        "hki,hkj->hij",
        columns,
        lax.all_gather(right_loc, "blk", axis=1, tiled=True),
        preferred_element_type=jnp.float32,
    )
    returned_prod = lax.all_to_all(
        total.astype(jnp.bfloat16), ("ch", "sub"), split_axis=1, concat_axis=0, tiled=True
    )
    prod = jnp.transpose(returned_prod, (1, 2, 0)).astype(jnp.float32)
    mid, inverse_mid = norm_parts(prod)
    y_low = (mid * gain_mid + bias_mid).astype(jnp.bfloat16)
    flat_y = y_low.reshape(rows * width, hidden)
    outp = jnp.dot(flat_y, w_out, preferred_element_type=jnp.float32).reshape(rows, width, chan)
    upstream = pair_grad.astype(jnp.float32)
    d_out = (upstream * sig_g).astype(jnp.bfloat16)
    d_sig = upstream * outp
    flat_d = d_out.reshape(rows * width, chan)
    dw_out_part = jnp.dot(flat_y.T, flat_d, preferred_element_type=jnp.float32)
    d_mid = jnp.dot(flat_d, w_out.T, preferred_element_type=jnp.float32).reshape(
        rows, width, hidden
    )
    dgain_mid_part = jnp.sum(d_mid * mid, axis=(0, 1))
    dbias_mid_part = jnp.sum(d_mid, axis=(0, 1))
    mid_totals = lax.psum((dw_out_part, dgain_mid_part, dbias_mid_part), ("blk", "ch", "sub"))
    d_prod = norm_back(d_mid * gain_mid, mid, inverse_mid).astype(jnp.bfloat16)
    d_groups = lax.all_to_all(
        jnp.transpose(d_prod, (2, 0, 1)), ("ch", "sub"), split_axis=0, concat_axis=1, tiled=True
    )
    piece = lax.all_gather(d_groups, "blk", axis=1, tiled=True)
    part_left = jnp.einsum("hkj,hij->hki", right_loc, piece, preferred_element_type=jnp.float32)
    grad_left = part_left
    grad_right = jnp.einsum("hki,hij->hkj", left_loc, piece, preferred_element_type=jnp.float32)
    grad_left, grad_right = (grad_left, grad_right)
    both_grads = jnp.stack([grad_left, grad_right]).astype(jnp.bfloat16)
    returned_grads = lax.all_to_all(
        both_grads, ("ch", "sub"), split_axis=2, concat_axis=1, tiled=True
    )
    pair_grads = jnp.transpose(returned_grads, (0, 2, 3, 1)).astype(jnp.float32)
    grad_a = pair_grads[0]
    grad_b = pair_grads[1]
    d_gate_a = grad_a * maskf * val_a * sig_a * (1.0 - sig_a)
    d_val_a = grad_a * maskf * sig_a
    d_gate_b = grad_b * maskf * val_b * sig_b * (1.0 - sig_b)
    d_val_b = grad_b * maskf * sig_b
    d_gate_g = d_sig * sig_g * (1.0 - sig_g)
    d_proj = jnp.concatenate([d_gate_a, d_val_a, d_gate_b, d_val_b, d_gate_g], axis=-1).astype(
        jnp.bfloat16
    )
    flat_p = d_proj.reshape(rows * width, -1)
    dw_in_part = jnp.dot(flat_x.T, flat_p, preferred_element_type=jnp.float32)
    d_x = jnp.dot(flat_p, w_in.T, preferred_element_type=jnp.float32).reshape(rows, width, chan)
    dgain_in_part = jnp.sum(d_x * normed, axis=(0, 1))
    dbias_in_part = jnp.sum(d_x, axis=(0, 1))
    d_pair = norm_back(d_x * gain_in, normed, inverse).astype(jnp.bfloat16)
    scale = 1.0 / width
    in_totals = lax.psum((dw_in_part, dgain_in_part, dbias_in_part), ("blk", "ch", "sub"))
    sums = (in_totals[0], in_totals[1], in_totals[2], mid_totals[0], mid_totals[1], mid_totals[2])
    return (
        d_pair,
        sums[0] * scale,
        sums[3] * scale,
        sums[1] * scale,
        sums[2] * scale,
        sums[4] * scale,
        sums[5] * scale,
    )


MESH = pl.DeviceIdType.MESH
PAD = 16
VMEM_BYTES = 58 * 1024 * 1024


def flat_slot(sizes, blk, ch, sub):
    return (blk * sizes[1] + ch) * sizes[2] + sub


def lane_mean(values):
    return jnp.mean(values, axis=-1, keepdims=True)


def norm_rows(values):
    center = values - lane_mean(values)
    inverse = lax.rsqrt(lane_mean(center * center) + 1e-05)
    return center * inverse, inverse


def sigm(values):
    return 0.5 * jnp.tanh(0.5 * values) + 0.5


def dot_t(left, right):
    return lax.dot_general(left, right, (((1,), (1,)), ((), ())), preferred_element_type=jnp.float32)


def t_dot(left, right):
    return lax.dot_general(left, right, (((0,), (0,)), ((), ())), preferred_element_type=jnp.float32)


def outer_sum(length, row_of, vec_of, width, chan, block):
    step = 8

    def body(t, acc):
        acc = list(acc)
        for s in range(step):
            q = t * step + s
            vec = vec_of(q)
            for p in range(block):
                acc[p] = acc[p] + row_of(p, q) * vec
        return tuple(acc)

    zero = jnp.zeros((width, chan), jnp.float32)
    return lax.fori_loop(0, length // step, body, (zero,) * block)


def front_kernel(
    sizes, rows, width,
    act_hbm, grad_hbm, mask_hbm, w_in_hbm, w_out_hbm, vec_hbm,
    xs, nrm, fa, fb, ca, cb, qa, qb, dp, dpg, dw_out_ref, dgain_mid_ref, dbias_mid_ref,
    ga, gg, mask_ref, w_in_ref, w_out_ref, vec_refs, sg, ys, dos, in_sem, send_sem, recv_sem, core_send,
):
    nz, nx, nc = sizes
    chips = nz * nx
    pairs = rows * width
    chan = w_out_ref.shape[1]
    hid = w_out_ref.shape[0]
    scale = 1.0 / width
    z, x, c = lax.axis_index("blk"), lax.axis_index("ch"), lax.axis_index("sub")
    y = lax.axis_index("grp")
    me = flat_slot(sizes, z, x, c)
    barrier = pltpu.get_barrier_semaphore()
    others = [
        (lax.rem(z + s, nz), lax.rem(x + r, nx))
        for r in range(nx) for s in range(nz) if s or r
    ]
    peers = [(y, zz, xx, c) for zz, xx in others]
    cores = [(y, z, x, lax.rem(c + s, nc)) for s in range(1, nc)]
    for peer in peers + cores:
        pl.semaphore_signal(barrier, inc=1, device_id=peer, device_id_type=MESH)
    loads = [
        pltpu.make_async_copy(act_hbm, ga.at[me, pl.ds(0, pairs)], in_sem.at[0]),
        pltpu.make_async_copy(mask_hbm, mask_ref, in_sem.at[1]),
        pltpu.make_async_copy(grad_hbm, gg.at[me], in_sem.at[2]),
        pltpu.make_async_copy(w_in_hbm, w_in_ref, in_sem.at[3]),
        pltpu.make_async_copy(w_out_hbm, w_out_ref, in_sem.at[4]),
    ] + [
        pltpu.make_async_copy(src, dst, in_sem.at[5 + n])
        for n, (src, dst) in enumerate(zip(vec_hbm, vec_refs))
    ]
    for load in loads:
        load.start()
    loads[1].wait()
    ga[me, pairs:, :] = jnp.zeros((PAD, chan), jnp.bfloat16)
    mine = mask_ref[...].astype(jnp.float32)
    ga[me, pairs:, :width] = jnp.concatenate(
        [jnp.broadcast_to(mine[r : r + 1, :], (PAD // rows, width)) for r in range(rows)], axis=0
    ).astype(jnp.bfloat16)
    loads[0].wait()
    pl.semaphore_wait(barrier, len(peers) + len(cores))

    bufs = (ga, gg)

    def chip_copy(which, slot, n, peer):
        return pltpu.make_async_remote_copy(
            src_ref=bufs[which].at[slot], dst_ref=bufs[which].at[slot],
            send_sem=send_sem.at[which, n], recv_sem=recv_sem.at[which, slot],
            device_id=peer, device_id_type=MESH,
        )

    def core_copy(which, slot, n):
        return pltpu.make_async_remote_copy(
            src_ref=bufs[which].at[slot], dst_ref=bufs[which].at[slot],
            send_sem=core_send.at[which, n], recv_sem=recv_sem.at[which, slot],
            device_id=cores[n // chips], device_id_type=MESH,
        )

    def send_own(which):
        for n, peer in enumerate(peers):
            chip_copy(which, me, n, peer).start()
        for k in range(nc - 1):
            core_copy(which, me, k * chips).start()

    def take(which, n):
        zz, xx = others[n - 1]
        slot = flat_slot(sizes, zz, xx, c)
        chip_copy(which, slot, 0, peers[0]).wait_recv()
        for k in range(nc - 1):
            core_copy(which, slot, k * chips + n).start()

    def take_core(which, slot):
        chip_copy(which, slot, 0, peers[0]).wait_recv()

    send_own(0)
    loads[2].wait()
    send_own(1)
    for load in loads[5:]:
        load.wait()
    gain_in, bias_in, gain_mid, bias_mid = [ref[...] for ref in vec_refs]
    at_row = lax.broadcasted_iota(jnp.int32, (width, chan), 0)
    at_lane = lax.broadcasted_iota(jnp.int32, (width, chan), 1)
    on_diag = at_row == at_lane
    ones = jnp.ones((chan, chan), jnp.bfloat16)

    def project(slots):
        act = jnp.concatenate([ga[s, :pairs, :] for s in slots], axis=0)
        lines = [ga[s, pairs:, :].astype(jnp.float32) for s in slots]
        diag = [
            jnp.where(on_diag, jnp.broadcast_to(line[r * (PAD // rows)][None, :], (width, chan)), 0.0)
            for line in lines for r in range(rows)
        ]
        mask = jnp.dot(
            jnp.concatenate(diag, axis=0).astype(jnp.bfloat16), ones,
            preferred_element_type=jnp.float32,
        )
        normed, _ = norm_rows(act.astype(jnp.float32))
        x_low = (normed * gain_in + bias_in).astype(jnp.bfloat16)

        def put(ref, value):
            for p, s in enumerate(slots):
                ref[pl.ds(pl.multiple_of(s * pairs, pairs), pairs), :] = value[
                    p * pairs : (p + 1) * pairs
                ]

        put(nrm, normed)
        put(xs, x_low)
        proj = jnp.dot(x_low, w_in_ref[...], preferred_element_type=jnp.float32)
        for at, fac, coef, gate in ((0, fa, ca, qa), (2, fb, cb, qb)):
            sig = sigm(proj[:, at * hid : (at + 1) * hid])
            val = proj[:, (at + 1) * hid : (at + 2) * hid]
            masked = mask * sig
            full = masked * val
            put(fac, full.astype(jnp.bfloat16).astype(jnp.float32))
            put(coef, masked)
            put(gate, full * (1.0 - sig))
        put(sg, sigm(proj[:, 4 * hid :]))

    loads[3].wait()
    for n in range(1, nz):
        take(0, n)
    for r in range(nx):
        if r:
            for n in range(r * nz, (r + 1) * nz):
                take(0, n)
        xx = lax.rem(x + r, nx)
        project([flat_slot(sizes, lax.rem(z + s, nz), xx, c) for s in range(nz)])
    for k in range(1, nc):
        cc = lax.rem(c + k, nc)
        for r in range(nx):
            xx = lax.rem(x + r, nx)
            slots = [flat_slot(sizes, lax.rem(z + s, nz), xx, cc) for s in range(nz)]
            for slot in slots:
                take_core(0, slot)
            project(slots)
    for n in range(1, chips):
        take(1, n)
    loads[4].wait()

    block = 8
    big = block * width

    def product(ib, carry):
        base = ib * block
        total = outer_sum(
            width,
            lambda p, k: fa[pl.ds(k * width + base + p, 1), :],
            lambda k: fb[pl.ds(pl.multiple_of(k * width, width), width), :],
            width, hid, block,
        )
        dp[pl.ds(pl.multiple_of(base * width, big), big), :] = jnp.concatenate(total, axis=0)
        return carry

    lax.fori_loop(0, width // block, product, 0)
    for k in range(1, nc):
        cc = lax.rem(c + k, nc)
        for zz, xx in [(z, x)] + others:
            take_core(1, flat_slot(sizes, zz, xx, cc))

    def middle(ib, sums):
        dgain, dbias = sums
        here = pl.ds(pl.multiple_of(ib * big, big), big)
        prod = dp[here, :].astype(jnp.bfloat16).astype(jnp.float32)
        mid, inverse = norm_rows(prod)
        y_low = (mid * gain_mid + bias_mid).astype(jnp.bfloat16)
        ys[here, :] = y_low
        per_block = block // rows
        upstream = jnp.concatenate(
            [gg[ib * per_block + s] for s in range(per_block)], axis=0
        ).astype(jnp.float32)
        sig = sg[here, :]
        outp = jnp.dot(y_low, w_out_ref[...], preferred_element_type=jnp.float32)
        d_out = (upstream * sig).astype(jnp.bfloat16)
        dos[here, :] = d_out
        dpg[here, :] = (upstream * outp * sig * (1.0 - sig)).astype(jnp.bfloat16)
        d_mid = dot_t(d_out, w_out_ref[...])
        dgain = dgain + jnp.sum(d_mid * mid, axis=0, keepdims=True)
        dbias = dbias + jnp.sum(d_mid, axis=0, keepdims=True)
        u = d_mid * gain_mid
        d_prod = inverse * (u - lane_mean(u) - mid * lane_mean(u * mid))
        dp[here, :] = d_prod.astype(jnp.bfloat16).astype(jnp.float32)
        return dgain, dbias

    none = jnp.zeros((1, hid), jnp.float32)
    dgain, dbias = lax.fori_loop(0, width // block, middle, (none, none))
    dgain_mid_ref[...] = dgain * scale
    dbias_mid_ref[...] = dbias * scale
    dw_out_ref[...] = t_dot(ys[...], dos[...]) * scale
    for which in (0, 1):
        for n, peer in enumerate(peers):
            chip_copy(which, me, n, peer).wait_send()
        for n in range((nc - 1) * chips):
            core_copy(which, me, n).wait_send()


def back_part(
    sizes, rows, width, xs, nrm, fa, fb, ca, cb, qa, qb, dp, dpg, ga, w_in_ref, gain_in_ref,
    d_pair_ref, dw_in_ref, dgain_in_ref, dbias_in_ref, dpr, dxs,
    part_out, part_in, vec_out, vec_in, half_send, half_recv,
):
    nc = sizes[2]
    pairs = rows * width
    hid, chan = fa.shape[1], nrm.shape[1]
    scale = 1.0 / width
    z, x, c = lax.axis_index("blk"), lax.axis_index("ch"), lax.axis_index("sub")
    me = flat_slot(sizes, z, x, c)
    other = (lax.axis_index("grp"), z, x, lax.rem(c + 1, nc))
    block = 8
    big = block * width
    per_block = block // rows
    blocks = width // block // nc

    def slot_rows(n):
        return pl.ds(pl.multiple_of((n * nc + c) * pairs, pairs), pairs)

    def back(kb, sums):
        dgain, dbias = sums
        here = pl.ds(pl.multiple_of(kb * big, big), big)

        def pick(ref):
            return jnp.concatenate(
                [ref[slot_rows(kb * per_block + q), :] for q in range(per_block)], axis=0
            )

        def line(p):
            return ((kb * per_block + p // rows) * nc + c) * pairs + (p % rows) * width

        left = outer_sum(
            width,
            lambda p, j: fb[pl.ds(line(p) + j, 1), :],
            lambda j: dp[pl.ds(j, width, stride=width), :],
            width, hid, block,
        )
        grad = jnp.concatenate(left, axis=0).astype(jnp.bfloat16).astype(jnp.float32)
        dpr[here, :hid] = (grad * pick(qa)).astype(jnp.bfloat16)
        dpr[here, hid : 2 * hid] = (grad * pick(ca)).astype(jnp.bfloat16)
        right = outer_sum(
            width,
            lambda p, i: fa[pl.ds(line(p) + i, 1), :],
            lambda i: dp[pl.ds(pl.multiple_of(i * width, width), width), :],
            width, hid, block,
        )
        grad = jnp.concatenate(right, axis=0).astype(jnp.bfloat16).astype(jnp.float32)
        dpr[here, 2 * hid : 3 * hid] = (grad * pick(qb)).astype(jnp.bfloat16)
        dpr[here, 3 * hid : 4 * hid] = (grad * pick(cb)).astype(jnp.bfloat16)
        dpr[here, 4 * hid :] = pick(dpg)
        d_x = dot_t(dpr[here, :], w_in_ref[...])
        dxs[here, :] = d_x
        dgain = dgain + jnp.sum(d_x * pick(nrm), axis=0, keepdims=True)
        dbias = dbias + jnp.sum(d_x, axis=0, keepdims=True)
        return dgain, dbias

    none = jnp.zeros((1, chan), jnp.float32)
    dgain, dbias = lax.fori_loop(0, blocks, back, (none, none))
    vec_out[0:8, :] = jnp.broadcast_to(dgain, (8, chan))
    vec_out[8:16, :] = jnp.broadcast_to(dbias, (8, chan))
    x_half = jnp.concatenate([xs[slot_rows(n), :] for n in range(sizes[0] * sizes[1])], axis=0)
    part_out[...] = t_dot(x_half, dpr[...]).astype(jnp.bfloat16)
    swaps = [
        pltpu.make_async_remote_copy(
            src_ref=src, dst_ref=dst, send_sem=half_send.at[n], recv_sem=half_recv.at[n],
            device_id=other, device_id_type=MESH,
        )
        for n, (src, dst) in enumerate(((part_out, part_in), (vec_out, vec_in)))
    ]
    for swap in swaps:
        swap.start()
    _, inverse = norm_rows(ga[me, :pairs, :].astype(jnp.float32))
    own = pl.ds(pl.multiple_of(me * pairs, pairs), pairs)
    kept = pl.ds(pl.multiple_of(me // nc * pairs, pairs), pairs)
    normed = nrm[own, :]
    v = dxs[kept, :] * gain_in_ref[...]
    d_pair_ref[...] = (inverse * (v - lane_mean(v) - normed * lane_mean(v * normed))).astype(
        jnp.bfloat16
    )
    for swap in swaps:
        swap.wait()
    dw_in_ref[...] = (
        part_out[...].astype(jnp.float32) + part_in[...].astype(jnp.float32)
    ) * scale
    dgain_in_ref[...] = (vec_out[0:1, :] + vec_in[0:1, :]) * scale
    dbias_in_ref[...] = (vec_out[8:9, :] + vec_in[8:9, :]) * scale


def whole_kernel(
    sizes, rows, width,
    act_hbm, grad_hbm, mask_hbm, w_in_hbm, w_out_hbm, gain_in_hbm, bias_in_hbm, gain_mid_hbm, bias_mid_hbm,
    d_pair_ref, dw_in_ref, dw_out_ref, dgain_in_ref, dbias_in_ref, dgain_mid_ref, dbias_mid_ref,
    xs, nrm, fa, fb, ca, cb, qa, qb, dp, dpg, dpr, dxs,
    ga, gg, mask_ref, w_in_ref, w_out_ref, gain_in_ref, bias_in_ref, gain_mid_ref, bias_mid_ref,
    sg, ys, dos, in_sem, send_sem, recv_sem, core_send,
    part_out, part_in, vec_out, vec_in, half_send, half_recv,
):
    front_kernel(
        sizes, rows, width, act_hbm, grad_hbm, mask_hbm, w_in_hbm, w_out_hbm,
        (gain_in_hbm, bias_in_hbm, gain_mid_hbm, bias_mid_hbm),
        xs, nrm, fa, fb, ca, cb, qa, qb, dp, dpg, dw_out_ref, dgain_mid_ref, dbias_mid_ref,
        ga, gg, mask_ref, w_in_ref, w_out_ref,
        (gain_in_ref, bias_in_ref, gain_mid_ref, bias_mid_ref),
        sg, ys, dos, in_sem, send_sem, recv_sem, core_send,
    )
    back_part(
        sizes, rows, width, xs, nrm, fa, fb, ca, cb, qa, qb, dp, dpg, ga, w_in_ref, gain_in_ref,
        d_pair_ref, dw_in_ref, dgain_in_ref, dbias_in_ref, dpr, dxs,
        part_out, part_in, vec_out, vec_in, half_send, half_recv,
    )


def finish_kernel(count, *refs):
    sems = refs[-1]
    loads = [
        pltpu.make_async_copy(refs[n], refs[2 * count + n], sems.at[0, n]) for n in range(count)
    ]
    stores = [
        pltpu.make_async_copy(refs[2 * count + n], refs[count + n], sems.at[1, n])
        for n in range(count)
    ]
    for load in loads:
        load.start()
    for load, store in zip(loads, stores):
        load.wait()
        store.start()
    for store in stores:
        store.wait()


def fused(sizes, pair_act, pair_grad, pair_mask, w_in, w_out, gain_in, bias_in, gain_mid, bias_mid):
    rows, width, chan = pair_act.shape
    hid = w_out.shape[0]
    pairs = rows * width
    chips = sizes[0] * sizes[1]
    slots = chips * sizes[2]
    full = slots * pairs
    f32, low = jnp.float32, jnp.bfloat16
    vmem = pl.BlockSpec(memory_space=pltpu.VMEM)
    hbm = pl.BlockSpec(memory_space=pltpu.HBM)
    vector = jax.ShapeDtypeStruct((1, hid), f32)
    out = pl.pallas_call(
        functools.partial(whole_kernel, sizes, rows, width),
        out_shape=(
            jax.ShapeDtypeStruct((pairs, chan), low),
            jax.ShapeDtypeStruct(w_in.shape, f32),
            jax.ShapeDtypeStruct(w_out.shape, f32),
        ) + (vector,) * 4,
        in_specs=[hbm] * 9,
        out_specs=(vmem,) * 7,
        scratch_shapes=[pltpu.VMEM((full, chan), low)]
        + [pltpu.VMEM((full, hid), f32)] * 8
        + [
            pltpu.VMEM((full, hid), low),
            pltpu.VMEM((full // sizes[2], w_in.shape[1]), low),
            pltpu.VMEM((full // sizes[2], chan), f32),
            pltpu.VMEM((slots, pairs + PAD, chan), low),
            pltpu.VMEM((slots, pairs, chan), low),
            pltpu.VMEM((rows, width), jnp.int32),
            pltpu.VMEM(w_in.shape, low),
            pltpu.VMEM(w_out.shape, low),
        ]
        + [pltpu.VMEM((1, chan), f32)] * 4
        + [
            pltpu.VMEM((full, chan), f32),
            pltpu.VMEM((full, hid), low),
            pltpu.VMEM((full, chan), low),
            pltpu.SemaphoreType.DMA((9,)),
            pltpu.SemaphoreType.DMA((2, chips)),
            pltpu.SemaphoreType.DMA((2, slots)),
            pltpu.SemaphoreType.DMA((2, slots)),
            pltpu.VMEM(w_in.shape, low),
            pltpu.VMEM(w_in.shape, low),
            pltpu.VMEM((16, chan), f32),
            pltpu.VMEM((16, chan), f32),
            pltpu.SemaphoreType.DMA((2,)),
            pltpu.SemaphoreType.DMA((2,)),
        ],
        compiler_params=pltpu.CompilerParams(
            collective_id=0, has_side_effects=True, vmem_limit_bytes=VMEM_BYTES
        ),
    )(
        pair_act.reshape(pairs, chan), pair_grad.reshape(pairs, chan), pair_mask, w_in, w_out,
        gain_in.reshape(1, chan), bias_in.reshape(1, chan),
        gain_mid.reshape(1, hid), bias_mid.reshape(1, hid),
    )
    anywhere = pl.BlockSpec(memory_space=pl.ANY)
    out = pl.pallas_call(
        functools.partial(finish_kernel, len(out)),
        out_shape=tuple(jax.ShapeDtypeStruct(piece.shape, piece.dtype) for piece in out),
        in_specs=[anywhere] * len(out),
        out_specs=(anywhere,) * len(out),
        scratch_shapes=[pltpu.VMEM(piece.shape, piece.dtype) for piece in out]
        + [pltpu.SemaphoreType.DMA((2, len(out)))],
        compiler_params=pltpu.CompilerParams(vmem_limit_bytes=VMEM_BYTES),
    )(*out)
    return (out[0].reshape(rows, width, chan), out[1], out[2]) + tuple(
        piece.reshape(-1) for piece in out[3:]
    )


def choose(mesh, *args):
    rows, width, chan = args[0].shape
    sizes = (mesh.shape["blk"], mesh.shape["ch"], mesh.shape["sub"])
    fits = width * width * chan * 128 <= VMEM_BYTES
    whole = sizes[2] == 2 and width % 32 == 0 and 8 % rows == 0 and chan >= width and chan == 128 and args[4].shape[0] == 128
    if fits and whole and rows * sizes[0] * sizes[1] * sizes[2] == width:
        return fused(sizes, *args)
    return shards(*args)


def solution(mesh):
    in_specs = (
        P(("grp", "blk", "ch", "sub"), None, None),
        P(("grp", "blk", "ch", "sub"), None, None),
        P(("grp", "blk", "ch", "sub"), None),
        P(),
        P(),
        P(),
        P(),
        P(),
        P(),
    )
    out_specs = (
        P(("grp", "blk", "ch", "sub"), None, None),
        P("grp", None),
        P("grp", None),
        P("grp"),
        P("grp"),
        P("grp"),
        P("grp"),
    )
    body = functools.partial(choose, mesh)
    return jax.shard_map(body, mesh=mesh, in_specs=in_specs, out_specs=out_specs, check_vma=False)
```
